512 devices in a mesh: batch: 64 (over y, z), tile: 8 (over x, core).
Axes of the slice: x: 4, y: 4, z: 16, core: 2. Of those that a mesh axis runs over, the one named last changes fastest.
Arguments:
- first_view_output: bfloat16 [4096, 4096], P('batch', 'tile'), may hold values from -900 to 900
- second_view_output: bfloat16 [4096, 4096], P('batch', 'tile'), may hold values from -900 to 900
Outputs:
- gradient_first_view: bfloat16 [4096, 4096], P('batch', 'tile')
- gradient_second_view: bfloat16 [4096, 4096], P('batch', 'tile')
- loss: float32 [], replicated
The draws below stay inside these ranges and needn't reach their ends.
All inputs are finite; a program needn't handle non-finite values.
Results may differ from the reference program's by a relative error of at most 0.0054.
Values may be sent and summed in bfloat16 or wider, within the bound.
A program may use at most 64 MiB of HBM per device.

```python
import math
import jax
import jax.numpy as jnp
from jax import lax

E = 4096
B = 4096
N_TILE = 8


def shared_field(key, row_high, latent_scale):
    subkeys = jax.random.split(key, 4)
    common = jax.random.normal(subkeys[0], (B, E), jnp.float32)
    latent = jax.random.normal(subkeys[1], (B, 4), jnp.float32)
    loading = jax.random.normal(subkeys[2], (4, E), jnp.float32) * latent_scale
    for factor in range(4):
        common = common + latent[:, factor:factor + 1] * loading[factor:factor + 1, :]
    row_scale = jnp.exp(jax.random.uniform(subkeys[3], (B, 1), jnp.float32, 0.0, math.log(row_high)))
    return (common, row_scale)


def block_position():
    block_width = E // N_TILE
    return ((jnp.arange(E, dtype=jnp.int32) % block_width).astype(jnp.float32) / block_width)[None, :]


def draw_first_view_output(key, part):
    common, row_scale = shared_field(key, 3.0, 0.3)
    key = jax.random.fold_in(key, 11)
    subkeys = jax.random.split(key, 3)
    noise = jax.random.normal(subkeys[0], (B, E), jnp.float32) * 0.6
    feature_scale = jnp.exp(jax.random.uniform(subkeys[1], (1, E), jnp.float32, math.log(0.5), math.log(5.0)))
    shift = jax.random.normal(subkeys[2], (1, E), jnp.float32) * 0.5 * feature_scale
    values = (common + noise) * row_scale * feature_scale + shift
    return jnp.clip(values, -900.0, 900.0).astype(jnp.bfloat16)


def draw_second_view_output(key, part):
    common, row_scale = shared_field(key, 3.0, 0.3)
    key = jax.random.fold_in(key, 23)
    subkeys = jax.random.split(key, 3)
    position = block_position()
    noise = jax.random.normal(subkeys[0], (B, E), jnp.float32) * 0.3 * jnp.exp(position * math.log(10.0))
    feature_scale = jnp.exp(jax.random.uniform(subkeys[1], (1, E), jnp.float32, math.log(0.5), math.log(5.0)))
    shift = jax.random.normal(subkeys[2], (1, E), jnp.float32) * 0.5 * feature_scale
    values = (common + noise) * row_scale * feature_scale + shift
    return jnp.clip(values, -900.0, 900.0).astype(jnp.bfloat16)


def setup_inputs(seed: int = 0) -> dict:
    streams_of = jax.random.split(jax.random.key(seed), 3)
    return {
        "first_view_output": draw_first_view_output(jax.random.fold_in(streams_of[2], 71), 0),
        "second_view_output": draw_second_view_output(jax.random.fold_in(streams_of[2], 71), 0),
    }


epsilon = 1e-05
off_weight = 0.0051

def batch_standardize(values):
    widened = values.astype(jnp.float32)
    centre = lax.optimization_barrier(jnp.mean(widened, axis=0))
    centred = widened - centre
    spread = lax.optimization_barrier(jnp.mean(centred * centred, axis=0))
    inverse_deviation = lax.rsqrt(spread + epsilon)
    return (centred * inverse_deviation, inverse_deviation)

def batch_norm_backward(incoming_gradient, standardized_input, inverse_deviation):
    first_input = lax.optimization_barrier(jnp.mean(incoming_gradient, axis=0))
    second_input = lax.optimization_barrier(jnp.mean(incoming_gradient * standardized_input, axis=0))
    return ((incoming_gradient - first_input - standardized_input * second_input) * inverse_deviation).astype(jnp.bfloat16)

def reference(first_view_output, second_view_output):
    standardized_first, inverse_deviation_first = batch_standardize(first_view_output)
    standardized_second, inverse_deviation_second = batch_standardize(second_view_output)
    normed_first_view = standardized_first.astype(jnp.bfloat16)
    normed_second_view = standardized_second.astype(jnp.bfloat16)
    corr = jnp.dot(normed_first_view.T, normed_second_view, preferred_element_type=jnp.float32) / B
    identity = jnp.eye(E, dtype=bool)
    loss = jnp.sum(jnp.where(identity, (1.0 - corr) * (1.0 - corr), off_weight * corr * corr)) / E
    grad_corr = jnp.where(identity, -2.0 * (1.0 - corr), 2.0 * off_weight * corr).astype(jnp.bfloat16)
    backward_first_view = jnp.dot(normed_second_view, grad_corr.T, preferred_element_type=jnp.float32)
    backward_second_view = jnp.dot(normed_first_view, grad_corr, preferred_element_type=jnp.float32)
    gradient_first_view = batch_norm_backward(backward_first_view, standardized_first, inverse_deviation_first)
    gradient_second_view = batch_norm_backward(backward_second_view, standardized_second, inverse_deviation_second)
    return (gradient_first_view, gradient_second_view, loss)
```

```python
import jax
import jax.numpy as jnp
from jax import lax
from jax.experimental import pallas as pl
from jax.experimental.pallas import tpu as pltpu
from jax.sharding import PartitionSpec as P

epsilon = 1e-05
off_weight = 0.0051
SIDE = 4
DEPTH = 16
ROWS = 64
LANE = 128
MESH = pl.DeviceIdType.MESH


def kernel(
    x1, x2, o1, o2, loss_ref,
    stage, gath, nbuf, oth, stat, cross, tail, coef,
    ksend, arecv, bsend, brecv, csend, kfull, acc, gout, outs, lbx, lby,
    ssem, misc, grecv, asem, bsem, csem, dsem,
):
    n, nz, rows = SIDE, DEPTH, ROWS
    group = n * rows
    width = 2 * LANE
    apiece, bpiece = group // n, group // (n * n)
    half = nz // 2
    features = float(n * n * width)
    b, t = lax.axis_index("batch"), lax.axis_index("tile")
    y, z = b // nz, lax.rem(b, nz)
    x, c = t // 2, lax.rem(t, 2)

    def dev(x, c, y, z):
        return (y * nz + z, x * 2 + c)

    def xp(d):
        return lax.rem(x + d, n)

    def yp(d):
        return lax.rem(y + d, n)

    def zp(d):
        return lax.rem(z + d + nz, nz)

    def send(src, dst, out, into, to):
        pltpu.make_async_remote_copy(
            src_ref=src, dst_ref=dst, send_sem=out, recv_sem=into,
            device_id=to, device_id_type=MESH,
        ).start()

    def arrive(ref, sem):
        pltpu.make_async_copy(ref, ref, sem).wait()

    barrier = pltpu.get_barrier_semaphore()
    peers = 0
    for dc in range(2):
        for d in range(n):
            if d or dc:
                cc = lax.rem(c + dc, 2)
                pl.semaphore_signal(barrier, 1, device_id=dev(x, cc, yp(d), z), device_id_type=MESH)
                peers += 1
            if d:
                cc = lax.rem(c + dc, 2)
                pl.semaphore_signal(barrier, 1, device_id=dev(xp(d), cc, y, z), device_id_type=MESH)
                peers += 1
    for d in range(1, nz):
        pl.semaphore_signal(barrier, 1, device_id=dev(x, c, y, zp(d)), device_id_type=MESH)
        peers += 1
    for q in range(n):
        stage[0, q] = x1[:, q * LANE:(q + 1) * LANE]
        stage[1, q] = x2[:, q * LANE:(q + 1) * LANE]
    acc[...] = jnp.zeros_like(acc)
    pl.semaphore_wait(barrier, peers)

    for dc in range(2):
        for d in range(n):
            if d or dc:
                v, yy = lax.rem(c + dc, 2), yp(d)
                send(stage.at[v, yy], gath.at[z, c * n + y], ssem.at[0], misc.at[0], dev(x, v, yy, z))
    gath[z, c * n + y] = stage[c, y]
    arrive(gath.at[z, pl.ds(0, 2 * n - 1)], misc.at[0])

    def block_of(way, s):
        return zp(-s) if way == 0 else zp(s)

    def forward(way, s, h):
        part = gath.at[block_of(way, s), pl.ds(h * n, n)]
        to = zp(1) if way == 0 else zp(-1)
        send(part, part, ssem.at[1], grecv.at[way, s, h], dev(x, c, y, to))

    for h in range(2):
        for way in range(2):
            forward(way, 0, h)

    def centre(block, h, q):
        return gath[block, h * n + q].astype(jnp.float32)

    for h in range(2):
        cols = slice(h * LANE, (h + 1) * LANE)
        total = jnp.zeros((1, LANE), jnp.float32)
        for q in range(n):
            total += jnp.sum(centre(z, h, q), axis=0, keepdims=True)
        mean = total / group
        spread = jnp.zeros((1, LANE), jnp.float32)
        for q in range(n):
            v = centre(z, h, q) - mean
            spread += jnp.sum(v * v, axis=0, keepdims=True)
        stat[z, 0:1, cols] = mean
        stat[z, 1:2, cols] = spread
    for d in range(1, nz):
        send(stat.at[z], stat.at[z], ssem.at[2], misc.at[1], dev(x, c, y, zp(d)))
    arrive(stat.at[pl.ds(0, nz - 1)], misc.at[1])
    mean = jnp.zeros((1, width), jnp.float32)
    for q in range(nz):
        mean += stat[q, 0:1, :]
    mean = mean / nz
    spread = jnp.zeros((1, width), jnp.float32)
    for q in range(nz):
        v = stat[q, 0:1, :] - mean
        spread += stat[q, 1:2, :] + group * (v * v)
    coef[0:1, :] = mean
    coef[1:2, :] = lax.rsqrt(spread / (group * nz) + epsilon)

    def standard(block, h, q):
        cols = slice(h * LANE, (h + 1) * LANE)
        return (centre(block, h, q) - coef[0:1, cols]) * coef[1:2, cols]

    def normalize(block):
        for h in range(2):
            for q in range(n):
                nbuf[block, q * rows:(q + 1) * rows, h * LANE:(h + 1) * LANE] = standard(
                    block, h, q
                ).astype(jnp.bfloat16)

    normalize(z)
    send(nbuf.at[z], oth, ssem.at[3], misc.at[2], dev(x, 1 - c, y, z))

    def peer(axis, d, cc):
        return dev(xp(d), cc, y, z) if axis == 0 else dev(x, cc, yp(d), z)

    def step(i, carry):
        for h in range(2):
            for way in range(2):
                last = half if h == way else half - 1

                @pl.when((i >= 1) & (i <= last))
                def _():
                    arrive(gath.at[block_of(way, i), pl.ds(h * n, n)], grecv.at[way, i - 1, h])

                @pl.when((i >= 1) & (i <= last - 1))
                def _():
                    forward(way, i, h)

        for k in range(2):
            first, second = (0, 1) if k == 0 else (1, 0)
            at_first, at_second = (x, y) if k == 0 else (y, x)

            j = i - k

            @pl.when((j >= 0) & (j < half))
            def _():
                block = block_of(k, i)

                @pl.when(i > 0)
                def _():
                    normalize(block)

                ksend[k, j] = lax.dot_general(
                    nbuf[z], nbuf[block], (((1,), (1,)), ((), ())),
                    preferred_element_type=jnp.float32,
                ).astype(jnp.bfloat16).reshape(n, apiece, group)
                for d in range(1, n):
                    to = lax.rem(at_first + d, n)
                    send(ksend.at[k, j, to], arecv.at[k, j, d - 1], ssem.at[4], asem.at[k, j], peer(first, d, c))

            j1 = i - k - 1

            @pl.when((j1 >= 0) & (j1 < half))
            def _():
                arrive(arecv.at[k, j1], asem.at[k, j1])
                s = ksend[k, j1, at_first].astype(jnp.float32)
                for d in range(n - 1):
                    s += arecv[k, j1, d].astype(jnp.float32)
                bsend[k, j1] = s.astype(jnp.bfloat16).reshape(n, bpiece, group)
                for d in range(1, n):
                    to = lax.rem(at_second + d, n)
                    send(bsend.at[k, j1, to], brecv.at[k, j1, d - 1], ssem.at[5], bsem.at[k, j1], peer(second, d, c))

            j2 = i - k - 2

            @pl.when((j2 >= 0) & (j2 < half))
            def _():
                arrive(brecv.at[k, j2], bsem.at[k, j2])
                s = bsend[k, j2, at_second].astype(jnp.float32)
                for d in range(n - 1):
                    s += brecv[k, j2, d].astype(jnp.float32)
                csend[k, j2] = s.astype(jnp.bfloat16)
                for d in range(n):
                    send(csend.at[k, j2], kfull.at[k, j2, at_first, at_second], ssem.at[6], csem.at[k, j2], peer(second, d, 1 - c))

            j3 = i - k - 3

            @pl.when((j3 >= 0) & (j3 < half))
            def _():
                arrive(kfull.at[k, j3, at_first], csem.at[k, j3])
                for d in range(1, n):
                    send(kfull.at[k, j3, at_first], kfull.at[k, j3, at_first], ssem.at[7], dsem.at[k, j3], peer(first, d, c))

            j4 = i - k - 4

            @pl.when((j4 >= 0) & (j4 < half))
            def _():
                arrive(arecv.at[k, j4], dsem.at[k, j4])
                acc[...] += jnp.dot(
                    kfull[k, j4].reshape(group, group), nbuf[block_of(k, i - 4)],
                    preferred_element_type=jnp.float32,
                )

        @pl.when(i == 2)
        def _():
            arrive(oth, misc.at[2])
            for h in range(2):
                cols = slice(h * LANE, (h + 1) * LANE)
                sums = [jnp.zeros((1, LANE), jnp.float32)] * 3
                for q in range(n):
                    lines = slice(q * rows, (q + 1) * rows)
                    theirs = oth[lines, cols].astype(jnp.float32)
                    ours = nbuf[z, lines, cols].astype(jnp.float32)
                    for m, v in enumerate((theirs, theirs * standard(z, h, q), theirs * ours)):
                        sums[m] = sums[m] + jnp.sum(v, axis=0, keepdims=True)
                for m in range(3):
                    cross[z, m:m + 1, cols] = sums[m]
                cross[z, 3:4, cols] = jnp.zeros((1, LANE), jnp.float32)
            for d in range(1, nz):
                send(cross.at[z], cross.at[z], ssem.at[8], misc.at[3], dev(x, c, y, zp(d)))

        return carry

    lax.fori_loop(0, half + 5, step, 0)

    for h in range(2):
        cols = slice(h * LANE, (h + 1) * LANE)
        plain = jnp.zeros((1, LANE), jnp.float32)
        times = jnp.zeros((1, LANE), jnp.float32)
        for q in range(n):
            v = acc[q * rows:(q + 1) * rows, cols]
            plain += jnp.sum(v, axis=0, keepdims=True)
            times += jnp.sum(v * standard(z, h, q), axis=0, keepdims=True)
        tail[z, 0:1, cols] = plain
        tail[z, 1:2, cols] = times
    for d in range(1, nz):
        send(tail.at[z], tail.at[z], ssem.at[9], misc.at[4], dev(x, c, y, zp(d)))
    arrive(cross.at[pl.ds(0, nz - 1)], misc.at[3])
    mixed = cross[0]
    for q in range(1, nz):
        mixed += cross[q]
    total_rows = float(group * nz)
    mixed = mixed / total_rows
    diagonal = mixed[2:3, :]
    scale = 2.0 * off_weight / total_rows
    lead = -2.0 * (1.0 - diagonal) - 2.0 * off_weight * diagonal
    arrive(tail.at[pl.ds(0, nz - 1)], misc.at[4])
    sums = tail[0]
    for q in range(1, nz):
        sums += tail[q]
    sums = sums / total_rows
    coef[2:3, :] = lead
    coef[3:4, :] = scale * sums[0:1, :] + lead * mixed[0:1, :]
    coef[4:5, :] = scale * sums[1:2, :] + lead * mixed[1:2, :]

    terms = (1.0 - diagonal) * (1.0 - diagonal) + off_weight * (
        sums[1:2, :] / total_rows - diagonal * diagonal
    )
    mine = jnp.sum(terms, axis=1, keepdims=True) * (0.5 / features)
    lbx[t] = jnp.broadcast_to(mine, (1, LANE))
    for dc in range(2):
        for d in range(n):
            if d:
                send(lbx.at[t], lbx.at[t], ssem.at[10], misc.at[5], dev(xp(d), lax.rem(c + dc, 2), y, z))
    send(lbx.at[t], lbx.at[t], ssem.at[10], misc.at[5], dev(x, 1 - c, y, z))

    for h in range(2):
        cols = slice(h * LANE, (h + 1) * LANE)
        for q in range(n):
            lines = slice(q * rows, (q + 1) * rows)
            back = scale * acc[lines, cols] + coef[2:3, cols] * oth[lines, cols].astype(jnp.float32)
            g = (back - coef[3:4, cols] - standard(z, h, q) * coef[4:5, cols]) * coef[1:2, cols]
            gout[h * n + q] = g.astype(jnp.bfloat16)
    for dc in range(2):
        for d in range(n):
            if d or dc:
                v, yy = lax.rem(c + dc, 2), yp(d)
                send(gout.at[v * n + yy], outs.at[c, y], ssem.at[11], misc.at[6], dev(x, v, yy, z))
    outs[c, y] = gout[c * n + y]

    arrive(lbx.at[pl.ds(0, 2 * n - 1)], misc.at[5])
    part = lbx[0]
    for q in range(1, 2 * n):
        part += lbx[q]
    lby[y] = part
    for d in range(1, n):
        send(lby.at[y], lby.at[y], ssem.at[12], misc.at[7], dev(x, c, yp(d), z))

    arrive(gath.at[0, pl.ds(0, 2 * n - 1)], misc.at[6])
    for q in range(n):
        o1[:, q * LANE:(q + 1) * LANE] = outs[0, q]
        o2[:, q * LANE:(q + 1) * LANE] = outs[1, q]
    arrive(lby.at[pl.ds(0, n - 1)], misc.at[7])
    part = lby[0]
    for q in range(1, n):
        part += lby[q]
    loss_ref[...] = part

    arrive(gath.at[0, pl.ds(0, 2 * n - 1)], ssem.at[0])
    arrive(gath.at[pl.ds(0, nz - 1)], ssem.at[1])
    arrive(stat.at[pl.ds(0, nz - 1)], ssem.at[2])
    arrive(oth, ssem.at[3])
    arrive(arecv, ssem.at[4])
    arrive(brecv, ssem.at[5])
    arrive(bsend, ssem.at[6])
    arrive(arecv, ssem.at[7])
    arrive(cross.at[pl.ds(0, nz - 1)], ssem.at[8])
    arrive(tail.at[pl.ds(0, nz - 1)], ssem.at[9])
    arrive(lbx.at[pl.ds(0, 2 * n - 1)], ssem.at[10])
    arrive(gath.at[0, pl.ds(0, 2 * n - 1)], ssem.at[11])
    arrive(lby.at[pl.ds(0, n - 1)], ssem.at[12])


def local(first_view_output, second_view_output):
    n, nz, rows = SIDE, DEPTH, ROWS
    group, width, half = n * rows, 2 * LANE, nz // 2
    apiece, bpiece = group // n, group // (n * n)
    bf16, f32 = jnp.bfloat16, jnp.float32
    shape = first_view_output.shape
    vmem = pl.BlockSpec(memory_space=pltpu.VMEM)
    g1, g2, loss = pl.pallas_call(
        kernel,
        out_shape=(
            jax.ShapeDtypeStruct(shape, bf16),
            jax.ShapeDtypeStruct(shape, bf16),
            jax.ShapeDtypeStruct((1, LANE), f32),
        ),
        in_specs=[vmem] * 2,
        out_specs=(vmem,) * 3,
        scratch_shapes=[
            pltpu.VMEM((2, n, rows, LANE), bf16),
            pltpu.VMEM((nz, 2 * n, rows, LANE), bf16),
            pltpu.VMEM((nz, group, width), bf16),
            pltpu.VMEM((group, width), bf16),
            pltpu.VMEM((nz, 2, width), f32),
            pltpu.VMEM((nz, 4, width), f32),
            pltpu.VMEM((nz, 2, width), f32),
            pltpu.VMEM((8, width), f32),
            pltpu.VMEM((2, half, n, apiece, group), bf16),
            pltpu.VMEM((2, half, n - 1, apiece, group), bf16),
            pltpu.VMEM((2, half, n, bpiece, group), bf16),
            pltpu.VMEM((2, half, n - 1, bpiece, group), bf16),
            pltpu.VMEM((2, half, bpiece, group), bf16),
            pltpu.VMEM((2, half, n, n, bpiece, group), bf16),
            pltpu.VMEM((group, width), f32),
            pltpu.VMEM((2 * n, rows, LANE), bf16),
            pltpu.VMEM((2, n, rows, LANE), bf16),
            pltpu.VMEM((2 * n, 1, LANE), f32),
            pltpu.VMEM((n, 1, LANE), f32),
            pltpu.SemaphoreType.DMA((13,)),
            pltpu.SemaphoreType.DMA((8,)),
            pltpu.SemaphoreType.DMA((2, half, 2)),
            pltpu.SemaphoreType.DMA((2, half)),
            pltpu.SemaphoreType.DMA((2, half)),
            pltpu.SemaphoreType.DMA((2, half)),
            pltpu.SemaphoreType.DMA((2, half)),
        ],
        compiler_params=pltpu.CompilerParams(
            collective_id=0, has_side_effects=True, vmem_limit_bytes=40 * 2**20
        ),
    )(first_view_output, second_view_output)
    return g1, g2, loss[0, 0]


def solution(mesh):
    spec = P("batch", "tile")
    return jax.shard_map(
        local, mesh=mesh, in_specs=(spec, spec), out_specs=(spec, spec, P()), check_vma=False
    )
```

```python
import jax
import jax.numpy as jnp
from jax import lax
from jax.experimental import pallas as pl
from jax.experimental.pallas import tpu as pltpu
from jax.sharding import PartitionSpec as P

epsilon = 1e-05
off_weight = 0.0051
SIDE = 4
DEPTH = 16
ROWS = 64
COLS = 512
LANE = 128
LAG = 3
RING = 5
MESH = pl.DeviceIdType.MESH
f32, bf16 = jnp.float32, jnp.bfloat16


def kernel(
    x1, x2, o1, o2, loss_ref,
    own, gath, lraw, nl, nr, stl, sty, stz, mr, coef,
    ksend, arecv, dsend, kfull, acc, tl, ty, ysend, yrecv, total, gout, outs, lbx,
    ssem, misc, grecv, asem, dsem,
):
    n, nz, rows = SIDE, DEPTH, ROWS
    hr = rows // 2
    group = n * rows
    width = 2 * COLS
    half = nz // 2
    all_rows = float(group * nz)
    features = float(n * width)
    b, t = lax.axis_index("batch"), lax.axis_index("tile")
    y, z = b // nz, lax.rem(b, nz)
    x, c = t // 2, lax.rem(t, 2)

    def dev(x, c, y, z):
        return (y * nz + z, x * 2 + c)

    def xp(d):
        return lax.rem(x + d, n)

    def yp(d):
        return lax.rem(y + d, n)

    def zp(d):
        return lax.rem(z + d + nz, nz)

    def send(src, dst, out, into, to):
        pltpu.make_async_remote_copy(
            src_ref=src, dst_ref=dst, send_sem=out, recv_sem=into,
            device_id=to, device_id_type=MESH,
        ).start()

    def arrive(ref, sem):
        pltpu.make_async_copy(ref, ref, sem).wait()

    far = sorted(range(1, nz), key=lambda d: -min(d, nz - d))

    barrier = pltpu.get_barrier_semaphore()
    peers = 0
    for d in far:
        pl.semaphore_signal(barrier, 1, device_id=dev(x, c, y, zp(d)), device_id_type=MESH)
        peers += 1
    for dc in range(2):
        for d in range(n):
            cc = lax.rem(c + dc, 2)
            if d or dc:
                pl.semaphore_signal(barrier, 1, device_id=dev(x, cc, yp(d), z), device_id_type=MESH)
                peers += 1
            if d:
                pl.semaphore_signal(barrier, 1, device_id=dev(xp(d), cc, y, z), device_id_type=MESH)
                peers += 1

    for r in range(2):
        lines = slice(r * hr, (r + 1) * hr)
        own[0, c, r] = x1[lines, :]
        own[1, c, r] = x2[lines, :]
        gath[z, 2 * c + r] = own[c, c, r]
    for q in range(n):
        cols = slice(q * LANE, (q + 1) * LANE)
        v1, v2 = x1[:, cols].astype(f32), x2[:, cols].astype(f32)
        a1 = jnp.sum(v1, axis=0, keepdims=True) / rows
        a2 = jnp.sum(v2, axis=0, keepdims=True) / rows
        v1, v2 = v1 - a1, v2 - a2
        stl[q, 0:1, :] = a1
        stl[q, 1:2, :] = a2
        stl[q, 2:3, :] = jnp.sum(v1 * v1, axis=0, keepdims=True)
        stl[q, 3:4, :] = jnp.sum(v2 * v2, axis=0, keepdims=True)
        stl[q, 4:5, :] = jnp.sum(v1 * v2, axis=0, keepdims=True)
        stl[q, 5:8, :] = jnp.zeros((3, LANE), f32)
    sty[y] = stl[y]
    acc[...] = jnp.zeros_like(acc)
    pl.semaphore_wait(barrier, peers)

    for v in range(2):
        send(own.at[v, c], own.at[v, c], ssem.at[0], misc.at[0], dev(x, 1 - c, y, z))
    for d in range(1, n):
        send(stl.at[yp(d)], sty.at[y], ssem.at[1], misc.at[1], dev(x, c, yp(d), z))

    def block_of(way, s):
        return zp(-s) if way == 0 else zp(s)

    def piece(i):
        return lax.rem(2 * c + i, 4)

    def forward(way, s, i):
        part = gath.at[block_of(way, s), piece(i)]
        to = zp(1) if way == 0 else zp(-1)
        send(part, part, ssem.at[2], grecv.at[way, s, i], dev(x, c, y, to))

    def ring(s, pieces):
        for i in pieces:
            for way in range(2):
                last = half if i // 2 == way else half - 1

                @pl.when(s <= last)
                def _():
                    arrive(gath.at[block_of(way, s), piece(i)], grecv.at[way, s - 1, i])

                @pl.when(s <= last - 1)
                def _():
                    forward(way, s, i)

    for i in range(2):
        for way in range(2):
            forward(way, 0, i)
    arrive(own.at[0], misc.at[0])
    for r in range(2):
        gath[z, 2 * (1 - c) + r] = own[c, 1 - c, r]
    for i in range(2, 4):
        for way in range(2):
            forward(way, 0, i)
    for d in range(1, n):
        send(gath.at[z], lraw.at[y], ssem.at[3], misc.at[2], dev(x, c, yp(d), z))
    for i in range(4):
        lraw[y, i] = gath[z, i]

    def combine(ref, parts, count):
        means = ref[0, 0:2, :]
        for q in range(1, parts):
            means += ref[q, 0:2, :]
        means = means / parts
        m1, m2 = means[0:1, :], means[1:2, :]
        s1 = s2 = s12 = jnp.zeros((1, LANE), f32)
        for q in range(parts):
            d1, d2 = ref[q, 0:1, :] - m1, ref[q, 1:2, :] - m2
            s1 += ref[q, 2:3, :] + count * (d1 * d1)
            s2 += ref[q, 3:4, :] + count * (d2 * d2)
            s12 += ref[q, 4:5, :] + count * (d1 * d2)
        return m1, m2, s1, s2, s12

    arrive(sty.at[pl.ds(0, n - 1)], misc.at[1])
    for r, v in enumerate(combine(sty, n, float(rows))):
        stz[z, r:r + 1, :] = v
    stz[z, 5:8, :] = jnp.zeros((3, LANE), f32)
    for d in far:
        send(stz.at[z], stz.at[z], ssem.at[4], misc.at[3], dev(x, c, y, zp(d)))
    for s in range(1, RING - 1):
        ring(s, range(4))
    arrive(stz.at[pl.ds(0, nz - 1)], misc.at[3])
    m1, m2, s1, s2, s12 = combine(stz, nz, float(group))
    i1 = lax.rsqrt(s1 / all_rows + epsilon)
    i2 = lax.rsqrt(s2 / all_rows + epsilon)
    mine = c * n + y
    for r, v in enumerate((m1, m2, i1, i2, s12 * i1 * i2 / all_rows)):
        mr[mine, r:r + 1, :] = v
    mr[mine, 5:8, :] = jnp.zeros((3, LANE), f32)
    for dc in range(2):
        for d in range(n):
            if d or dc:
                send(mr.at[mine], mr.at[mine], ssem.at[5], misc.at[4], dev(x, lax.rem(c + dc, 2), yp(d), z))
    ring(RING - 1, range(4))
    arrive(mr.at[pl.ds(0, 2 * n - 1)], misc.at[4])
    first = c == 0
    for q in range(2 * n):
        cols = slice(q * LANE, (q + 1) * LANE)
        for r, (u, v) in enumerate(((0, 1), (2, 3), (1, 0), (3, 2), (4, 4))):
            coef[r:r + 1, cols] = jnp.where(first, mr[q, u:u + 1, :], mr[q, v:v + 1, :])

    def standard(raw, h, r):
        cols = slice(h * COLS, (h + 1) * COLS)
        return (raw.astype(f32) - coef[r:r + 1, cols]) * coef[r + 1:r + 2, cols]

    arrive(lraw.at[pl.ds(0, n - 1)], misc.at[2])
    for q in range(n):
        for i in range(4):
            h, r = i // 2, i % 2
            nl[q * rows + r * hr:q * rows + (r + 1) * hr, h * COLS:(h + 1) * COLS] = standard(
                lraw[q, i], h, 0
            ).astype(bf16)

    def step(p, carry):
        ring(p + RING, range(2))

        @pl.when(p < half)
        def _():
            for k in range(2):
                block = zp(-p) if k == 0 else zp(p + 1)
                for i in range(4):
                    h, r = i // 2, i % 2
                    nr[p, k * rows + r * hr:k * rows + (r + 1) * hr, h * COLS:(h + 1) * COLS] = (
                        standard(gath[block, i], h, 0).astype(bf16)
                    )
            ksend[p] = lax.dot_general(
                nl[...], nr[p], (((1,), (1,)), ((), ())), preferred_element_type=f32
            ).astype(bf16).reshape(n, rows, 2 * rows)
            for d in range(1, n):
                send(ksend.at[p, xp(d)], arecv.at[p, d - 1], ssem.at[6], asem.at[p], dev(xp(d), c, y, z))

        ring(p + RING, range(2, 4))
        p1 = p - LAG

        @pl.when((p1 >= 0) & (p1 < half))
        def _():
            arrive(arecv.at[p1], asem.at[p1])
            s = ksend[p1, x].astype(f32)
            for d in range(n - 1):
                s += arecv[p1, d].astype(f32)
            dsend[p1] = s.astype(bf16)
            for d in range(n):
                send(dsend.at[p1], kfull.at[p1, x], ssem.at[7], dsem.at[p1], dev(xp(d), 1 - c, y, z))

        p2 = p - 2 * LAG

        @pl.when(p2 >= 0)
        def _():
            arrive(kfull.at[p2], dsem.at[p2])
            acc[...] += jnp.dot(
                kfull[p2].reshape(group, 2 * rows), nr[p2], preferred_element_type=f32
            ).reshape(n, rows, width)

        return carry

    lax.fori_loop(0, half + 2 * LAG, step, 0)

    plain = jnp.zeros((1, width), f32)
    times = jnp.zeros((1, width), f32)
    for q in range(n):
        v = acc[q]
        plain += jnp.sum(v, axis=0, keepdims=True)
        times += jnp.sum(v * nl[q * rows:(q + 1) * rows, :].astype(f32), axis=0, keepdims=True)
    tl[z, 0:1, :] = plain
    tl[z, 1:2, :] = times
    for d in far:
        send(tl.at[z], tl.at[z], ssem.at[8], misc.at[5], dev(x, c, y, zp(d)))
    for q in range(n):
        ysend[q] = acc[q].astype(bf16)
    for d in range(1, n):
        send(ysend.at[yp(d)], yrecv.at[d - 1], ssem.at[9], misc.at[6], dev(x, c, yp(d), z))
    arrive(tl.at[pl.ds(0, nz - 1)], misc.at[5])
    sums = tl[0]
    for q in range(1, nz):
        sums += tl[q]
    ty[y] = sums
    for d in range(1, n):
        send(ty.at[y], ty.at[y], ssem.at[10], misc.at[7], dev(x, c, yp(d), z))

    arrive(yrecv, misc.at[6])
    v = acc[y]
    for d in range(n - 1):
        v += yrecv[d].astype(f32)
    total[...] = v
    arrive(ty.at[pl.ds(0, n - 1)], misc.at[7])
    sums = ty[0]
    for q in range(1, n):
        sums += ty[q]
    sums = sums / all_rows
    diagonal = coef[4:5, :]
    scale = 2.0 * off_weight / all_rows
    lead = -2.0 * (1.0 - diagonal) - 2.0 * off_weight * diagonal

    terms = (1.0 - diagonal) * (1.0 - diagonal) + off_weight * (
        sums[1:2, :] / all_rows - diagonal * diagonal
    )
    lbx[t] = jnp.broadcast_to(
        jnp.sum(terms, axis=1, keepdims=True) * (0.5 / features), (1, LANE)
    )
    for dc in range(2):
        for d in range(n):
            if d or dc:
                send(lbx.at[t], lbx.at[t], ssem.at[11], misc.at[8], dev(xp(d), lax.rem(c + dc, 2), y, z))

    coef[5:6, :] = lead
    coef[6:7, :] = scale * sums[0:1, :]
    coef[7:8, :] = scale * sums[1:2, :] + lead * diagonal
    for h in range(2):
        cols = slice(h * COLS, (h + 1) * COLS)
        for r in range(2):
            lines = slice(r * hr, (r + 1) * hr)
            ours, theirs = standard(own[c, h, r], h, 0), standard(own[1 - c, h, r], h, 2)
            back = scale * total[lines, cols] + coef[5:6, cols] * theirs
            g = (back - coef[6:7, cols] - ours * coef[7:8, cols]) * coef[1:2, cols]
            gout[h, lines, :] = g.astype(bf16)
    send(gout.at[1 - c], outs.at[c], ssem.at[12], misc.at[9], dev(x, 1 - c, y, z))
    outs[c] = gout[c]
    arrive(outs.at[1 - c], misc.at[9])
    o1[...] = outs[0]
    o2[...] = outs[1]
    arrive(lbx.at[pl.ds(0, 2 * n - 1)], misc.at[8])
    part = lbx[0]
    for q in range(1, 2 * n):
        part += lbx[q]
    loss_ref[...] = part

    arrive(own.at[0], ssem.at[0])
    arrive(sty.at[pl.ds(0, n - 1)], ssem.at[1])
    arrive(gath.at[pl.ds(0, nz - 1)], ssem.at[2])
    arrive(lraw.at[pl.ds(0, n - 1)], ssem.at[3])
    arrive(stz.at[pl.ds(0, nz - 1)], ssem.at[4])
    arrive(mr.at[pl.ds(0, 2 * n - 1)], ssem.at[5])
    arrive(arecv, ssem.at[6])
    arrive(kfull, ssem.at[7])
    arrive(tl.at[pl.ds(0, nz - 1)], ssem.at[8])
    arrive(yrecv, ssem.at[9])
    arrive(ty.at[pl.ds(0, n - 1)], ssem.at[10])
    arrive(lbx.at[pl.ds(0, 2 * n - 1)], ssem.at[11])
    arrive(outs.at[0], ssem.at[12])


def local(first_view_output, second_view_output):
    n, nz, rows = SIDE, DEPTH, ROWS
    group, width, half = n * rows, 2 * COLS, nz // 2
    shape = first_view_output.shape
    vmem = pl.BlockSpec(memory_space=pltpu.VMEM)
    dma = pltpu.SemaphoreType.DMA
    g1, g2, loss = pl.pallas_call(
        kernel,
        out_shape=(
            jax.ShapeDtypeStruct(shape, bf16),
            jax.ShapeDtypeStruct(shape, bf16),
            jax.ShapeDtypeStruct((1, LANE), f32),
        ),
        in_specs=[vmem] * 2,
        out_specs=(vmem,) * 3,
        scratch_shapes=[
            pltpu.VMEM((2, 2, 2, rows // 2, COLS), bf16),
            pltpu.VMEM((nz, 4, rows // 2, COLS), bf16),
            pltpu.VMEM((n, 4, rows // 2, COLS), bf16),
            pltpu.VMEM((group, width), bf16),
            pltpu.VMEM((half, 2 * rows, width), bf16),
            pltpu.VMEM((n, 8, LANE), f32),
            pltpu.VMEM((n, 8, LANE), f32),
            pltpu.VMEM((nz, 8, LANE), f32),
            pltpu.VMEM((2 * n, 8, LANE), f32),
            pltpu.VMEM((8, width), f32),
            pltpu.VMEM((half, n, rows, 2 * rows), bf16),
            pltpu.VMEM((half, n - 1, rows, 2 * rows), bf16),
            pltpu.VMEM((half, rows, 2 * rows), bf16),
            pltpu.VMEM((half, n, rows, 2 * rows), bf16),
            pltpu.VMEM((n, rows, width), f32),
            pltpu.VMEM((nz, 2, width), f32),
            pltpu.VMEM((n, 2, width), f32),
            pltpu.VMEM((n, rows, width), bf16),
            pltpu.VMEM((n - 1, rows, width), bf16),
            pltpu.VMEM((rows, width), f32),
            pltpu.VMEM((2, rows, COLS), bf16),
            pltpu.VMEM((2, rows, COLS), bf16),
            pltpu.VMEM((2 * n, 1, LANE), f32),
            dma((13,)), dma((10,)), dma((2, half, 4)), dma((half,)), dma((half,)),
        ],
        compiler_params=pltpu.CompilerParams(
            collective_id=0, has_side_effects=True, vmem_limit_bytes=40 * 2**20
        ),
    )(first_view_output, second_view_output)
    return g1, g2, loss[0, 0]


def solution(mesh):
    spec = P("batch", "tile")
    return jax.shard_map(
        local, mesh=mesh, in_specs=(spec, spec), out_specs=(spec, spec, P()), check_vma=False
    )
```

```python
import jax
import jax.numpy as jnp
from jax import lax
from jax.experimental import pallas as pl
from jax.experimental.pallas import tpu as pltpu
from jax.sharding import PartitionSpec as P

epsilon = 1e-05
off_weight = 0.0051
SIDE = 4
DEPTH = 16
ROWS = 64
COLS = 512
LANE = 128
PIECES = 4
LAG = 4
RING = 5
MESH = pl.DeviceIdType.MESH
f32, bf16 = jnp.float32, jnp.bfloat16


def kernel(
    x1, x2, o1, o2, loss_ref,
    own, gath, lraw, nl, nr, stl, sty, stz, mr, coef,
    ksend, arecv, dsend, kfull, acc, tl, tsend, ty, ysend, yrecv, params, lbx,
    ssem, misc, grecv, asem, dsem, lsem,
):
    n, nz, rows = SIDE, DEPTH, ROWS
    np = PIECES // 2
    hr = rows // np
    group = n * rows
    width = 2 * COLS
    half = nz // 2
    all_rows = float(group * nz)
    features = float(n * width)
    b, t = lax.axis_index("batch"), lax.axis_index("tile")
    y, z = b // nz, lax.rem(b, nz)
    x, c = t // 2, lax.rem(t, 2)

    def dev(x, c, y, z):
        return (y * nz + z, x * 2 + c)

    def xp(d):
        return lax.rem(x + d, n)

    def yp(d):
        return lax.rem(y + d, n)

    def zp(d):
        return lax.rem(z + d + nz, nz)

    def send(src, dst, out, into, to):
        pltpu.make_async_remote_copy(
            src_ref=src, dst_ref=dst, send_sem=out, recv_sem=into,
            device_id=to, device_id_type=MESH,
        ).start()

    def arrive(ref, sem):
        pltpu.make_async_copy(ref, ref, sem).wait()

    far = sorted(range(1, nz), key=lambda d: -min(d, nz - d))

    barrier = pltpu.get_barrier_semaphore()
    peers = 0
    for d in far:
        pl.semaphore_signal(barrier, 1, device_id=dev(x, c, y, zp(d)), device_id_type=MESH)
        peers += 1
    plane = [(dx, dc, dy) for dx in range(n) for dc in range(2) for dy in range(n)][1:]
    for dx, dc, dy in plane:
        to = dev(xp(dx), lax.rem(c + dc, 2), yp(dy), z)
        pl.semaphore_signal(barrier, 1, device_id=to, device_id_type=MESH)
        peers += 1
    loads = [pltpu.make_async_copy(ref, own.at[v, c], lsem.at[v]) for v, ref in enumerate((x1, x2))]
    for load in loads:
        load.start()
    acc[...] = jnp.zeros_like(acc)

    for load in loads:
        load.wait()
    for r in range(np):
        gath[z, np * c + r] = own[c, c, r * hr:(r + 1) * hr, :]
    for q in range(n):
        cols = slice(q * LANE, (q + 1) * LANE)
        v1 = own[0, c, :, cols].astype(f32)
        v2 = own[1, c, :, cols].astype(f32)
        a1 = jnp.sum(v1, axis=0, keepdims=True) / rows
        a2 = jnp.sum(v2, axis=0, keepdims=True) / rows
        v1, v2 = v1 - a1, v2 - a2
        stl[q, 0:1, :] = a1
        stl[q, 1:2, :] = a2
        stl[q, 2:3, :] = jnp.sum(v1 * v1, axis=0, keepdims=True)
        stl[q, 3:4, :] = jnp.sum(v2 * v2, axis=0, keepdims=True)
        stl[q, 4:5, :] = jnp.sum(v1 * v2, axis=0, keepdims=True)
    sty[y] = stl[y]
    pl.semaphore_wait(barrier, peers)

    send(own.at[1 - c, c], own.at[1 - c, c], ssem.at[0], misc.at[0], dev(x, 1 - c, y, z))
    for d in range(1, n):
        send(stl.at[yp(d)], sty.at[y], ssem.at[1], misc.at[1], dev(x, c, yp(d), z))

    def block_of(way, s):
        return zp(-s) if way == 0 else zp(s)

    def piece(i):
        return lax.rem(np * c + i, 2 * np)

    def forward(way, s, i):
        part = gath.at[block_of(way, s), piece(i)]
        to = zp(1) if way == 0 else zp(-1)
        send(part, part, ssem.at[2], grecv.at[way, s, i], dev(x, c, y, to))

    def ring(u):
        s, g = u // 2, u % 2
        for k in range(np):
            i = np * g + k
            for way in range(2):
                last = half - g if way == 0 else half - 1 + g

                @pl.when(s <= last)
                def _():
                    arrive(gath.at[block_of(way, s), piece(i)], grecv.at[way, s - 1, i])

                @pl.when(s <= last - 1)
                def _():
                    forward(way, s, i)

    for i in range(np):
        for way in range(2):
            forward(way, 0, i)
    arrive(own.at[0, 0], misc.at[0])
    for r in range(np):
        gath[z, np * (1 - c) + r] = own[c, 1 - c, r * hr:(r + 1) * hr, :]
    for i in range(np, 2 * np):
        for way in range(2):
            forward(way, 0, i)
    for d in range(1, n):
        send(gath.at[z], lraw.at[y], ssem.at[3], misc.at[2], dev(x, c, yp(d), z))
    for i in range(2 * np):
        lraw[y, i] = gath[z, i]

    def combine(ref, parts, count):
        means = ref[0, 0:2, :]
        for q in range(1, parts):
            means += ref[q, 0:2, :]
        means = means / parts
        m1, m2 = means[0:1, :], means[1:2, :]
        s1 = s2 = s12 = jnp.zeros((1, LANE), f32)
        for q in range(parts):
            d1, d2 = ref[q, 0:1, :] - m1, ref[q, 1:2, :] - m2
            s1 += ref[q, 2:3, :] + count * (d1 * d1)
            s2 += ref[q, 3:4, :] + count * (d2 * d2)
            s12 += ref[q, 4:5, :] + count * (d1 * d2)
        return m1, m2, s1, s2, s12

    ring(2)
    arrive(sty.at[pl.ds(0, n - 1)], misc.at[1])
    for r, v in enumerate(combine(sty, n, float(rows))):
        stz[z, r:r + 1, :] = v
    for d in far:
        send(stz.at[z], stz.at[z], ssem.at[4], misc.at[3], dev(x, c, y, zp(d)))
    for u in range(3, 2 * RING - 2):
        ring(u)
    arrive(stz.at[pl.ds(0, nz - 1)], misc.at[3])
    m1, m2, s1, s2, s12 = combine(stz, nz, float(group))
    i1 = lax.rsqrt(s1 / all_rows + epsilon)
    i2 = lax.rsqrt(s2 / all_rows + epsilon)
    mine = c * n + y
    for r, v in enumerate((m1, m2, i1, i2, s12 * i1 * i2 / all_rows)):
        mr[mine, r:r + 1, :] = v
    for dc in range(2):
        for d in range(n):
            if d or dc:
                send(mr.at[mine], mr.at[mine], ssem.at[5], misc.at[4], dev(x, lax.rem(c + dc, 2), yp(d), z))
    ring(2 * RING - 2)
    ring(2 * RING - 1)
    arrive(mr.at[pl.ds(0, 2 * n - 1)], misc.at[4])
    first = c == 0
    for q in range(2 * n):
        cols = slice(q * LANE, (q + 1) * LANE)
        for r, (u, v) in enumerate(((0, 1), (2, 3), (4, 4))):
            coef[r:r + 1, cols] = jnp.where(first, mr[q, u:u + 1, :], mr[q, v:v + 1, :])

    def standard(raw, h):
        cols = slice(h * COLS, (h + 1) * COLS)
        return (raw.astype(f32) - coef[0:1, cols]) * coef[1:2, cols]

    arrive(lraw.at[pl.ds(0, n - 1)], misc.at[2])
    for q in range(n):
        for i in range(2 * np):
            h, r = i // np, i % np
            nl[q * rows + r * hr:q * rows + (r + 1) * hr, h * COLS:(h + 1) * COLS] = standard(
                lraw[q, i], h
            ).astype(bf16)

    def step(p, carry):
        ring(p + 2 * RING)

        @pl.when(p < half)
        def _():
            for k in range(2):
                block = zp(-p) if k == 0 else zp(p + 1)
                for i in range(2 * np):
                    h, r = i // np, i % np
                    nr[
                        p // 2,
                        pl.ds(pl.multiple_of(lax.rem(p, 2) * 2 * rows + k * rows + r * hr, hr), hr),
                        h * COLS:(h + 1) * COLS,
                    ] = (
                        standard(gath[block, i], h).astype(bf16)
                    )
            ksend[p] = lax.dot_general(
                nl[...], nr[p // 2, pl.ds(pl.multiple_of(lax.rem(p, 2) * 2 * rows, 2 * rows), 2 * rows), :],
                (((1,), (1,)), ((), ())), preferred_element_type=f32,
            ).astype(bf16).reshape(n, rows, 2 * rows)
            for d in range(1, n):
                send(ksend.at[p, xp(d)], arecv.at[p, d - 1], ssem.at[6], asem.at[p], dev(xp(d), c, y, z))

        p1 = p - LAG

        @pl.when((p1 >= 0) & (p1 < half))
        def _():
            arrive(arecv.at[p1], asem.at[p1])
            s = ksend[p1, x].astype(f32)
            for d in range(n - 1):
                s += arecv[p1, d].astype(f32)
            dsend[p1] = s.astype(bf16)
            for d in range(n):
                send(
                    dsend.at[p1],
                    kfull.at[p1 // 2, x, :, pl.ds(pl.multiple_of(lax.rem(p1, 2) * 2 * rows, 2 * rows), 2 * rows)],
                    ssem.at[7], dsem.at[p1 // 2], dev(xp(d), 1 - c, y, z),
                )

        p2 = p - 2 * LAG

        @pl.when((p2 >= 0) & (lax.rem(p2, 2) == 1))
        def _():
            two = p2 // 2
            arrive(kfull.at[two], dsem.at[two])
            acc[...] += jnp.dot(
                kfull[two].reshape(group, 4 * rows), nr[two], preferred_element_type=f32
            ).reshape(n, rows, width)

        return carry

    lax.fori_loop(0, half + 2 * LAG, step, 0)

    plain = jnp.zeros((1, width), f32)
    times = jnp.zeros((1, width), f32)
    for q in range(n):
        v = acc[q]
        plain += jnp.sum(v, axis=0, keepdims=True)
        times += jnp.sum(v * nl[q * rows:(q + 1) * rows, :].astype(f32), axis=0, keepdims=True)
    tl[z, 0:1, :] = plain
    tl[z, 1:2, :] = times
    for d in far:
        send(tl.at[z], tl.at[z], ssem.at[8], misc.at[5], dev(x, c, y, zp(d)))
    for q in range(n):
        for h in range(2):
            ysend[q, h] = acc[q, :, h * COLS:(h + 1) * COLS].astype(bf16)
    row = [(dc, d) for dc in range(2) for d in range(n)][1:]
    for dc, d in row:
        cc, yy = lax.rem(c + dc, 2), yp(d)
        send(ysend.at[yy, cc], yrecv.at[c * n + y], ssem.at[9], misc.at[6], dev(x, cc, yy, z))
    yrecv[c * n + y] = ysend[y, c]
    arrive(tl.at[pl.ds(0, nz - 1)], misc.at[5])
    sums = tl[0]
    for q in range(1, nz):
        sums += tl[q]
    for h in range(2):
        tsend[h] = sums[:, h * COLS:(h + 1) * COLS]
    for dc, d in row:
        cc, yy = lax.rem(c + dc, 2), yp(d)
        send(tsend.at[cc], ty.at[c * n + y], ssem.at[10], misc.at[7], dev(x, cc, yy, z))
    ty[c * n + y] = tsend[c]
    diagonal = coef[2:3, :]
    terms = ((1.0 - diagonal) * (1.0 - diagonal) - off_weight * diagonal * diagonal) / n + (
        off_weight / (all_rows * all_rows)
    ) * sums[1:2, :]
    place = t * n + y
    lbx[place] = jnp.broadcast_to(
        jnp.sum(terms, axis=1, keepdims=True) * (0.5 / features), (1, LANE)
    )
    for dx, dc, dy in plane:
        to = dev(xp(dx), lax.rem(c + dc, 2), yp(dy), z)
        send(lbx.at[place], lbx.at[place], ssem.at[11], misc.at[8], to)

    scale = 2.0 * off_weight / all_rows
    for q in range(n):
        cols = slice(q * LANE, (q + 1) * LANE)
        for r in range(5):
            params[r:r + 1, cols] = mr[c * n + q, r:r + 1, :]
    diagonal = params[4:5, :]
    lead = -2.0 * (1.0 - diagonal) - 2.0 * off_weight * diagonal
    hats = [
        (own[v, c].astype(f32) - params[v:v + 1, :]) * params[2 + v:3 + v, :] for v in range(2)
    ]
    arrive(yrecv.at[pl.ds(0, 2 * n - 1)], misc.at[6])
    arrive(ty.at[pl.ds(0, 2 * n - 1)], misc.at[7])
    for v, out in enumerate((o1, o2)):
        product = yrecv[v * n].astype(f32)
        sums = ty[v * n]
        for q in range(1, n):
            product += yrecv[v * n + q].astype(f32)
            sums += ty[v * n + q]
        sums = sums * (scale / all_rows)
        back = scale * product + lead * hats[1 - v]
        g = back - sums[0:1, :] - hats[v] * (sums[1:2, :] + lead * diagonal)
        out[...] = (g * params[2 + v:3 + v, :]).astype(bf16)
    arrive(lbx.at[pl.ds(0, 2 * n * n - 1)], misc.at[8])
    part = lbx[0]
    for q in range(1, 2 * n * n):
        part += lbx[q]
    loss_ref[...] = part

    arrive(own.at[0, 0], ssem.at[0])
    arrive(sty.at[pl.ds(0, n - 1)], ssem.at[1])
    arrive(gath.at[pl.ds(0, nz - 1)], ssem.at[2])
    arrive(lraw.at[pl.ds(0, n - 1)], ssem.at[3])
    arrive(stz.at[pl.ds(0, nz - 1)], ssem.at[4])
    arrive(mr.at[pl.ds(0, 2 * n - 1)], ssem.at[5])
    arrive(arecv, ssem.at[6])
    arrive(kfull, ssem.at[7])
    arrive(tl.at[pl.ds(0, nz - 1)], ssem.at[8])
    arrive(yrecv.at[pl.ds(0, 2 * n - 1)], ssem.at[9])
    arrive(ty.at[pl.ds(0, 2 * n - 1)], ssem.at[10])
    arrive(lbx.at[pl.ds(0, 2 * n * n - 1)], ssem.at[11])


def local(first_view_output, second_view_output):
    n, nz, rows = SIDE, DEPTH, ROWS
    group, width, half, np = n * rows, 2 * COLS, nz // 2, PIECES // 2
    shape = first_view_output.shape
    vmem = pl.BlockSpec(memory_space=pltpu.VMEM)
    dma = pltpu.SemaphoreType.DMA
    g1, g2, loss = pl.pallas_call(
        kernel,
        out_shape=(
            jax.ShapeDtypeStruct(shape, bf16),
            jax.ShapeDtypeStruct(shape, bf16),
            jax.ShapeDtypeStruct((1, LANE), f32),
        ),
        in_specs=[pl.BlockSpec(memory_space=pl.ANY)] * 2,
        out_specs=(vmem,) * 3,
        scratch_shapes=[
            pltpu.VMEM((2, 2, rows, COLS), bf16),
            pltpu.VMEM((nz, 2 * np, rows // np, COLS), bf16),
            pltpu.VMEM((n, 2 * np, rows // np, COLS), bf16),
            pltpu.VMEM((group, width), bf16),
            pltpu.VMEM((half // 2, 4 * rows, width), bf16),
            pltpu.VMEM((n, 5, LANE), f32),
            pltpu.VMEM((n, 5, LANE), f32),
            pltpu.VMEM((nz, 5, LANE), f32),
            pltpu.VMEM((2 * n, 5, LANE), f32),
            pltpu.VMEM((8, width), f32),
            pltpu.VMEM((half, n, rows, 2 * rows), bf16),
            pltpu.VMEM((half, n - 1, rows, 2 * rows), bf16),
            pltpu.VMEM((half, rows, 2 * rows), bf16),
            pltpu.VMEM((half // 2, n, rows, 4 * rows), bf16),
            pltpu.VMEM((n, rows, width), f32),
            pltpu.VMEM((nz, 2, width), f32),
            pltpu.VMEM((2, 2, COLS), f32),
            pltpu.VMEM((2 * n, 2, COLS), f32),
            pltpu.VMEM((n, 2, rows, COLS), bf16),
            pltpu.VMEM((2 * n, rows, COLS), bf16),
            pltpu.VMEM((8, COLS), f32),
            pltpu.VMEM((2 * n * n, 1, LANE), f32),
            dma((12,)), dma((9,)), dma((2, half, PIECES)), dma((half,)), dma((half,)), dma((2,)),
        ],
        compiler_params=pltpu.CompilerParams(
            collective_id=0, has_side_effects=True, vmem_limit_bytes=40 * 2**20
        ),
    )(first_view_output, second_view_output)
    return g1, g2, loss[0, 0]


def solution(mesh):
    spec = P("batch", "tile")
    return jax.shard_map(
        local, mesh=mesh, in_specs=(spec, spec), out_specs=(spec, spec, P()), check_vma=False
    )
```

```python
import jax
import jax.numpy as jnp
from jax import lax
from jax.experimental import pallas as pl
from jax.experimental.pallas import tpu as pltpu
from jax.sharding import PartitionSpec as P

epsilon = 1e-05
off_weight = 0.0051
SIDE = 4
DEPTH = 16
ROWS = 64
COLS = 512
LANE = 128
PIECES = 4
RING = 4
MESH = pl.DeviceIdType.MESH
f32, bf16 = jnp.float32, jnp.bfloat16


def kernel(
    x1, x2, o1, o2, loss_ref,
    own, gath, lraw, nl, nr, stl, sty, stz, mr, coef,
    ksend, arecv, dsend, kfull, klast, acc, tl, tsend, ty, ysend, yrecv, params, lbx,
    ssem, misc, grecv, asem, dsem, lsem, lastsem,
):
    n, nz, rows = SIDE, DEPTH, ROWS
    np = PIECES // 2
    hr = rows // np
    group = n * rows
    width = 2 * COLS
    half = nz // 2
    all_rows = float(group * nz)
    features = float(n * width)
    b, t = lax.axis_index("batch"), lax.axis_index("tile")
    y, z = b // nz, lax.rem(b, nz)
    x, c = t // 2, lax.rem(t, 2)

    def dev(x, c, y, z):
        return (y * nz + z, x * 2 + c)

    def xp(d):
        return lax.rem(x + d, n)

    def yp(d):
        return lax.rem(y + d, n)

    def zp(d):
        return lax.rem(z + d + nz, nz)

    def send(src, dst, out, into, to):
        pltpu.make_async_remote_copy(
            src_ref=src, dst_ref=dst, send_sem=out, recv_sem=into,
            device_id=to, device_id_type=MESH,
        ).start()

    def arrive(ref, sem):
        pltpu.make_async_copy(ref, ref, sem).wait()

    far = sorted(range(1, nz), key=lambda d: -min(d, nz - d))

    barrier = pltpu.get_barrier_semaphore()
    peers = 0
    for d in far:
        pl.semaphore_signal(barrier, 1, device_id=dev(x, c, y, zp(d)), device_id_type=MESH)
        peers += 1
    plane = [(dx, dc, dy) for dx in range(n) for dc in range(2) for dy in range(n)][1:]
    for dx, dc, dy in plane:
        to = dev(xp(dx), lax.rem(c + dc, 2), yp(dy), z)
        pl.semaphore_signal(barrier, 1, device_id=to, device_id_type=MESH)
        peers += 1
    loads = [pltpu.make_async_copy(ref, own.at[v, c], lsem.at[v]) for v, ref in enumerate((x1, x2))]
    for load in loads:
        load.start()
    acc[...] = jnp.zeros_like(acc)

    for load in loads:
        load.wait()
    for r in range(np):
        gath[z, np * c + r] = own[c, c, r * hr:(r + 1) * hr, :]
    for q in range(n):
        cols = slice(q * LANE, (q + 1) * LANE)
        v1 = own[0, c, :, cols].astype(f32)
        v2 = own[1, c, :, cols].astype(f32)
        a1 = jnp.sum(v1, axis=0, keepdims=True) / rows
        a2 = jnp.sum(v2, axis=0, keepdims=True) / rows
        v1, v2 = v1 - a1, v2 - a2
        stl[q, 0:1, :] = a1
        stl[q, 1:2, :] = a2
        stl[q, 2:3, :] = jnp.sum(v1 * v1, axis=0, keepdims=True)
        stl[q, 3:4, :] = jnp.sum(v2 * v2, axis=0, keepdims=True)
        stl[q, 4:5, :] = jnp.sum(v1 * v2, axis=0, keepdims=True)
    sty[y] = stl[y]
    pl.semaphore_wait(barrier, peers)

    def block_of(way, s):
        return zp(-s) if way == 0 else zp(s)

    def piece(i):
        return lax.rem(np * c + i, 2 * np)

    def forward(way, s, i):
        part = gath.at[block_of(way, s), piece(i)]
        to = zp(1) if way == 0 else zp(-1)
        send(part, part, ssem.at[2], grecv.at[way, s, i], dev(x, c, y, to))

    def ring(u):
        s, g = u // 2, u % 2
        for k in range(np):
            i = np * g + k
            for way in range(2):
                last = half - g if way == 0 else half - 1 + g

                @pl.when(s <= last)
                def _():
                    arrive(gath.at[block_of(way, s), piece(i)], grecv.at[way, s - 1, i])

                @pl.when(s <= last - 1)
                def _():
                    forward(way, s, i)

    send(own.at[1 - c, c], own.at[1 - c, c], ssem.at[0], misc.at[0], dev(x, 1 - c, y, z))
    for i in range(np):
        for way in range(2):
            forward(way, 0, i)
    for d in range(1, n):
        send(stl.at[yp(d)], sty.at[y], ssem.at[1], misc.at[1], dev(x, c, yp(d), z))
    arrive(own.at[0, 0], misc.at[0])
    for r in range(np):
        gath[z, np * (1 - c) + r] = own[c, 1 - c, r * hr:(r + 1) * hr, :]
    for i in range(np, 2 * np):
        for way in range(2):
            forward(way, 0, i)
    for d in range(1, n):
        send(gath.at[z], lraw.at[y], ssem.at[3], misc.at[2], dev(x, c, yp(d), z))
    for i in range(2 * np):
        lraw[y, i] = gath[z, i]

    def combine(ref, parts, count):
        means = ref[0, 0:2, :]
        for q in range(1, parts):
            means += ref[q, 0:2, :]
        means = means / parts
        m1, m2 = means[0:1, :], means[1:2, :]
        s1 = s2 = s12 = jnp.zeros((1, LANE), f32)
        for q in range(parts):
            d1, d2 = ref[q, 0:1, :] - m1, ref[q, 1:2, :] - m2
            s1 += ref[q, 2:3, :] + count * (d1 * d1)
            s2 += ref[q, 3:4, :] + count * (d2 * d2)
            s12 += ref[q, 4:5, :] + count * (d1 * d2)
        return m1, m2, s1, s2, s12

    ring(2)
    arrive(sty.at[pl.ds(0, n - 1)], misc.at[1])
    for r, v in enumerate(combine(sty, n, float(rows))):
        stz[z, r:r + 1, :] = v
    for d in far:
        send(stz.at[z], stz.at[z], ssem.at[4], misc.at[3], dev(x, c, y, zp(d)))
    for u in range(3, 2 * RING - 2):
        ring(u)
    arrive(stz.at[pl.ds(0, nz - 1)], misc.at[3])
    m1, m2, s1, s2, s12 = combine(stz, nz, float(group))
    i1 = lax.rsqrt(s1 / all_rows + epsilon)
    i2 = lax.rsqrt(s2 / all_rows + epsilon)
    mine = c * n + y
    for r, v in enumerate((m1, m2, i1, i2, s12 * i1 * i2 / all_rows)):
        mr[mine, r:r + 1, :] = v
    for dc in range(2):
        for d in range(n):
            if d or dc:
                send(mr.at[mine], mr.at[mine], ssem.at[5], misc.at[4], dev(x, lax.rem(c + dc, 2), yp(d), z))
    ring(2 * RING - 2)
    ring(2 * RING - 1)
    arrive(mr.at[pl.ds(0, 2 * n - 1)], misc.at[4])
    first = c == 0
    for q in range(2 * n):
        cols = slice(q * LANE, (q + 1) * LANE)
        for r, (u, v) in enumerate(((0, 1), (2, 3), (4, 4))):
            coef[r:r + 1, cols] = jnp.where(first, mr[q, u:u + 1, :], mr[q, v:v + 1, :])

    def standard(raw, h):
        cols = slice(h * COLS, (h + 1) * COLS)
        return (raw.astype(f32) - coef[0:1, cols]) * coef[1:2, cols]

    arrive(lraw.at[pl.ds(0, n - 1)], misc.at[2])
    for q in range(n):
        for i in range(2 * np):
            h, r = i // np, i % np
            nl[q * rows + r * hr:q * rows + (r + 1) * hr, h * COLS:(h + 1) * COLS] = standard(
                lraw[q, i], h
            ).astype(bf16)

    def multiply(p):
        place = pl.ds((p % 2) * 2 * rows, 2 * rows)
        for k in range(2):
            block = zp(-p) if k == 0 else zp(p + 1)
            for i in range(2 * np):
                h, r = i // np, i % np
                start = (p % 2) * 2 * rows + k * rows + r * hr
                nr[p // 2, start:start + hr, h * COLS:(h + 1) * COLS] = standard(
                    gath[block, i], h
                ).astype(bf16)
        ksend[p] = lax.dot_general(
            nl[...], nr[p // 2, place, :], (((1,), (1,)), ((), ())), preferred_element_type=f32
        ).astype(bf16).reshape(n, rows, 2 * rows)
        if p == half - 1:
            for d in range(n):
                send(ksend.at[p], klast.at[x], ssem.at[8], lastsem, dev(xp(d), 1 - c, y, z))
            return
        for d in range(1, n):
            send(ksend.at[p, xp(d)], arecv.at[p, d - 1], ssem.at[6], asem.at[p], dev(xp(d), c, y, z))

    def reduce(p):
        place = pl.ds((p % 2) * 2 * rows, 2 * rows)
        arrive(arecv.at[p], asem.at[p])
        s = ksend[p, x].astype(f32)
        for d in range(n - 1):
            s += arecv[p, d].astype(f32)
        dsend[p] = s.astype(bf16)
        for d in range(n):
            send(
                dsend.at[p], kfull.at[p // 2, x, :, place], ssem.at[7], dsem.at[p // 2],
                dev(xp(d), 1 - c, y, z),
            )

    def consume(two):
        arrive(kfull.at[two], dsem.at[two])
        acc[...] += jnp.dot(
            kfull[two].reshape(group, 4 * rows), nr[two], preferred_element_type=f32
        ).reshape(n, rows, width)

    def finish(p):
        k = p % 2
        if k == 0:
            arrive(kfull.at[p // 2, :, :, pl.ds(0, 2 * rows)], dsem.at[p // 2])
            s = kfull[p // 2, :, :, 0:2 * rows]
        else:
            arrive(klast, lastsem)
            s = klast[0].astype(f32)
            for d in range(1, n):
                s += klast[d].astype(f32)
            s = s.astype(bf16)
        acc[...] += jnp.dot(
            s.reshape(group, 2 * rows), nr[p // 2, k * 2 * rows:(k + 1) * 2 * rows, :],
            preferred_element_type=f32,
        ).reshape(n, rows, width)

    for work, p in (
        (ring, 8), (multiply, 0), (ring, 9), (multiply, 1), (ring, 10), (multiply, 2),
        (ring, 11), (multiply, 3), (reduce, 0), (ring, 12), (reduce, 1), (ring, 13),
        (multiply, 4), (multiply, 5), (ring, 14), (reduce, 2), (reduce, 3), (ring, 15),
        (multiply, 6), (consume, 0), (reduce, 4), (ring, 16), (ring, 17), (multiply, 7),
        (reduce, 5), (reduce, 6), (consume, 1), (consume, 2), (finish, 6), (finish, 7),
    ):
        work(p)

    plain = jnp.zeros((1, width), f32)
    times = jnp.zeros((1, width), f32)
    for q in range(n):
        v = acc[q]
        plain += jnp.sum(v, axis=0, keepdims=True)
        times += jnp.sum(v * nl[q * rows:(q + 1) * rows, :].astype(f32), axis=0, keepdims=True)
    tl[z, 0:1, :] = plain
    tl[z, 1:2, :] = times
    for d in far:
        send(tl.at[z], tl.at[z], ssem.at[9], misc.at[5], dev(x, c, y, zp(d)))
    for q in range(n):
        for h in range(2):
            ysend[q, h] = acc[q, :, h * COLS:(h + 1) * COLS].astype(bf16)
    row = [(dc, d) for dc in range(2) for d in range(n)][1:]
    for dc, d in row:
        cc, yy = lax.rem(c + dc, 2), yp(d)
        send(ysend.at[yy, cc], yrecv.at[c * n + y], ssem.at[10], misc.at[6], dev(x, cc, yy, z))
    yrecv[c * n + y] = ysend[y, c]
    arrive(tl.at[pl.ds(0, nz - 1)], misc.at[5])
    sums = tl[0]
    for q in range(1, nz):
        sums += tl[q]
    for h in range(2):
        tsend[h] = sums[:, h * COLS:(h + 1) * COLS]
    for dc, d in row:
        cc, yy = lax.rem(c + dc, 2), yp(d)
        send(tsend.at[cc], ty.at[c * n + y], ssem.at[11], misc.at[7], dev(x, cc, yy, z))
    ty[c * n + y] = tsend[c]
    diagonal = coef[2:3, :]
    terms = ((1.0 - diagonal) * (1.0 - diagonal) - off_weight * diagonal * diagonal) / n + (
        off_weight / (all_rows * all_rows)
    ) * sums[1:2, :]
    place = t * n + y
    lbx[place] = jnp.broadcast_to(
        jnp.sum(terms, axis=1, keepdims=True) * (0.5 / features), (1, LANE)
    )
    for dx, dc, dy in plane:
        to = dev(xp(dx), lax.rem(c + dc, 2), yp(dy), z)
        send(lbx.at[place], lbx.at[place], ssem.at[12], misc.at[8], to)

    scale = 2.0 * off_weight / all_rows
    for q in range(n):
        cols = slice(q * LANE, (q + 1) * LANE)
        for r in range(5):
            params[r:r + 1, cols] = mr[c * n + q, r:r + 1, :]
    diagonal = params[4:5, :]
    lead = -2.0 * (1.0 - diagonal) - 2.0 * off_weight * diagonal
    hats = [
        (own[v, c].astype(f32) - params[v:v + 1, :]) * params[2 + v:3 + v, :] for v in range(2)
    ]
    arrive(yrecv.at[pl.ds(0, 2 * n - 1)], misc.at[6])
    arrive(ty.at[pl.ds(0, 2 * n - 1)], misc.at[7])
    for v, out in enumerate((o1, o2)):
        product = yrecv[v * n].astype(f32)
        sums = ty[v * n]
        for q in range(1, n):
            product += yrecv[v * n + q].astype(f32)
            sums += ty[v * n + q]
        sums = sums * (scale / all_rows)
        back = scale * product + lead * hats[1 - v]
        g = back - sums[0:1, :] - hats[v] * (sums[1:2, :] + lead * diagonal)
        out[...] = (g * params[2 + v:3 + v, :]).astype(bf16)
    arrive(lbx.at[pl.ds(0, 2 * n * n - 1)], misc.at[8])
    part = lbx[0]
    for q in range(1, 2 * n * n):
        part += lbx[q]
    loss_ref[...] = part

    arrive(own.at[0, 0], ssem.at[0])
    arrive(sty.at[pl.ds(0, n - 1)], ssem.at[1])
    arrive(gath.at[pl.ds(0, nz - 1)], ssem.at[2])
    arrive(lraw.at[pl.ds(0, n - 1)], ssem.at[3])
    arrive(stz.at[pl.ds(0, nz - 1)], ssem.at[4])
    arrive(mr.at[pl.ds(0, 2 * n - 1)], ssem.at[5])
    arrive(arecv.at[pl.ds(0, half - 1)], ssem.at[6])
    arrive(ksend.at[pl.ds(0, half - 1)], ssem.at[7])
    arrive(klast, ssem.at[8])
    arrive(tl.at[pl.ds(0, nz - 1)], ssem.at[9])
    arrive(yrecv.at[pl.ds(0, 2 * n - 1)], ssem.at[10])
    arrive(ty.at[pl.ds(0, 2 * n - 1)], ssem.at[11])
    arrive(lbx.at[pl.ds(0, 2 * n * n - 1)], ssem.at[12])


def local(first_view_output, second_view_output):
    n, nz, rows = SIDE, DEPTH, ROWS
    group, width, half, np = n * rows, 2 * COLS, nz // 2, PIECES // 2
    shape = first_view_output.shape
    vmem = pl.BlockSpec(memory_space=pltpu.VMEM)
    dma = pltpu.SemaphoreType.DMA
    g1, g2, loss = pl.pallas_call(
        kernel,
        out_shape=(
            jax.ShapeDtypeStruct(shape, bf16),
            jax.ShapeDtypeStruct(shape, bf16),
            jax.ShapeDtypeStruct((1, LANE), f32),
        ),
        in_specs=[pl.BlockSpec(memory_space=pltpu.HBM)] * 2,
        out_specs=(vmem,) * 3,
        scratch_shapes=[
            pltpu.VMEM((2, 2, rows, COLS), bf16),
            pltpu.VMEM((nz, 2 * np, rows // np, COLS), bf16),
            pltpu.VMEM((n, 2 * np, rows // np, COLS), bf16),
            pltpu.VMEM((group, width), bf16),
            pltpu.VMEM((half // 2, 4 * rows, width), bf16),
            pltpu.VMEM((n, 5, LANE), f32),
            pltpu.VMEM((n, 5, LANE), f32),
            pltpu.VMEM((nz, 5, LANE), f32),
            pltpu.VMEM((2 * n, 5, LANE), f32),
            pltpu.VMEM((8, width), f32),
            pltpu.VMEM((half, n, rows, 2 * rows), bf16),
            pltpu.VMEM((half, n - 1, rows, 2 * rows), bf16),
            pltpu.VMEM((half, rows, 2 * rows), bf16),
            pltpu.VMEM((half // 2, n, rows, 4 * rows), bf16),
            pltpu.VMEM((n, n, rows, 2 * rows), bf16),
            pltpu.VMEM((n, rows, width), f32),
            pltpu.VMEM((nz, 2, width), f32),
            pltpu.VMEM((2, 2, COLS), f32),
            pltpu.VMEM((2 * n, 2, COLS), f32),
            pltpu.VMEM((n, 2, rows, COLS), bf16),
            pltpu.VMEM((2 * n, rows, COLS), bf16),
            pltpu.VMEM((8, COLS), f32),
            pltpu.VMEM((2 * n * n, 1, LANE), f32),
            dma((13,)), dma((9,)), dma((2, half, PIECES)), dma((half,)), dma((half,)), dma((2,)), dma,
        ],
        compiler_params=pltpu.CompilerParams(
            collective_id=0, has_side_effects=True, vmem_limit_bytes=40 * 2**20
        ),
    )(first_view_output, second_view_output)
    return g1, g2, loss[0, 0]


def solution(mesh):
    spec = P("batch", "tile")
    return jax.shard_map(
        local, mesh=mesh, in_specs=(spec, spec), out_specs=(spec, spec, P()), check_vma=False
    )
```

```python
import jax
import jax.numpy as jnp
from jax import lax
from jax.experimental import pallas as pl
from jax.experimental.pallas import tpu as pltpu
from jax.sharding import PartitionSpec as P

epsilon = 1e-05
off_weight = 0.0051
SIDE = 4
DEPTH = 16
ROWS = 64
COLS = 512
LANE = 128
PIECES = 4
RING = 4
MESH = pl.DeviceIdType.MESH
f32, bf16 = jnp.float32, jnp.bfloat16


def kernel(
    x1, x2, o1, o2, loss_ref,
    own, gath, lraw, nl, nr, stl, sty, stz, mr, coef,
    ksend, arecv, dsend, kfull, klast, kall, acc, tl, tsend, ty, ysend, yrecv, params, lbx,
    ssem, misc, grecv, asem, dsem, lsem, lastsem,
):
    n, nz, rows = SIDE, DEPTH, ROWS
    np = PIECES // 2
    hr = rows // np
    group = n * rows
    width = 2 * COLS
    half = nz // 2
    all_rows = float(group * nz)
    features = float(n * width)
    b, t = lax.axis_index("batch"), lax.axis_index("tile")
    y, z = b // nz, lax.rem(b, nz)
    x, c = t // 2, lax.rem(t, 2)

    def dev(x, c, y, z):
        return (y * nz + z, x * 2 + c)

    def xp(d):
        return lax.rem(x + d, n)

    def yp(d):
        return lax.rem(y + d, n)

    def zp(d):
        return lax.rem(z + d + nz, nz)

    def send(src, dst, out, into, to):
        pltpu.make_async_remote_copy(
            src_ref=src, dst_ref=dst, send_sem=out, recv_sem=into,
            device_id=to, device_id_type=MESH,
        ).start()

    def arrive(ref, sem):
        pltpu.make_async_copy(ref, ref, sem).wait()

    far = sorted(range(1, nz), key=lambda d: -min(d, nz - d))

    barrier = pltpu.get_barrier_semaphore()
    peers = 0
    for d in far:
        pl.semaphore_signal(barrier, 1, device_id=dev(x, c, y, zp(d)), device_id_type=MESH)
        peers += 1
    plane = [(dx, dc, dy) for dx in range(n) for dc in range(2) for dy in range(n)][1:]
    for dx, dc, dy in plane:
        to = dev(xp(dx), lax.rem(c + dc, 2), yp(dy), z)
        pl.semaphore_signal(barrier, 1, device_id=to, device_id_type=MESH)
        peers += 1
    loads = [pltpu.make_async_copy(ref, own.at[v, c], lsem.at[v]) for v, ref in enumerate((x1, x2))]
    for load in loads:
        load.start()
    acc[...] = jnp.zeros_like(acc)

    for load in loads:
        load.wait()
    for r in range(np):
        gath[z, np * c + r] = own[c, c, r * hr:(r + 1) * hr, :]
    for q in range(n):
        cols = slice(q * LANE, (q + 1) * LANE)
        v1 = own[0, c, :, cols].astype(f32)
        v2 = own[1, c, :, cols].astype(f32)
        a1 = jnp.sum(v1, axis=0, keepdims=True) / rows
        a2 = jnp.sum(v2, axis=0, keepdims=True) / rows
        v1, v2 = v1 - a1, v2 - a2
        stl[q, 0:1, :] = a1
        stl[q, 1:2, :] = a2
        stl[q, 2:3, :] = jnp.sum(v1 * v1, axis=0, keepdims=True)
        stl[q, 3:4, :] = jnp.sum(v2 * v2, axis=0, keepdims=True)
        stl[q, 4:5, :] = jnp.sum(v1 * v2, axis=0, keepdims=True)
    sty[y] = stl[y]
    pl.semaphore_wait(barrier, peers)

    def block_of(way, s):
        return zp(-s) if way == 0 else zp(s)

    def piece(i):
        return lax.rem(np * c + i, 2 * np)

    def forward(way, s, i):
        part = gath.at[block_of(way, s), piece(i)]
        to = zp(1) if way == 0 else zp(-1)
        send(part, part, ssem.at[2], grecv.at[way, s, i], dev(x, c, y, to))

    def ring(u):
        s, g = u // 2, u % 2
        for k in range(np):
            i = np * g + k
            for way in range(2):
                last = half - g if way == 0 else half - 1 + g

                @pl.when(s <= last)
                def _():
                    arrive(gath.at[block_of(way, s), piece(i)], grecv.at[way, s - 1, i])

                @pl.when(s <= last - 1)
                def _():
                    forward(way, s, i)

    send(own.at[1 - c, c], own.at[1 - c, c], ssem.at[0], misc.at[0], dev(x, 1 - c, y, z))
    for i in range(np):
        for way in range(2):
            forward(way, 0, i)
    for d in range(1, n):
        send(stl.at[yp(d)], sty.at[y], ssem.at[1], misc.at[1], dev(x, c, yp(d), z))
    arrive(own.at[0, 0], misc.at[0])
    for r in range(np):
        gath[z, np * (1 - c) + r] = own[c, 1 - c, r * hr:(r + 1) * hr, :]
    for i in range(np, 2 * np):
        for way in range(2):
            forward(way, 0, i)
    for d in range(1, n):
        send(gath.at[z], lraw.at[y], ssem.at[3], misc.at[2], dev(x, c, yp(d), z))
    for i in range(2 * np):
        lraw[y, i] = gath[z, i]

    def combine(ref, parts, count):
        means = ref[0, 0:2, :]
        for q in range(1, parts):
            means += ref[q, 0:2, :]
        means = means / parts
        m1, m2 = means[0:1, :], means[1:2, :]
        s1 = s2 = s12 = jnp.zeros((1, LANE), f32)
        for q in range(parts):
            d1, d2 = ref[q, 0:1, :] - m1, ref[q, 1:2, :] - m2
            s1 += ref[q, 2:3, :] + count * (d1 * d1)
            s2 += ref[q, 3:4, :] + count * (d2 * d2)
            s12 += ref[q, 4:5, :] + count * (d1 * d2)
        return m1, m2, s1, s2, s12

    arrive(sty.at[pl.ds(0, n - 1)], misc.at[1])
    for r, v in enumerate(combine(sty, n, float(rows))):
        stz[z, r:r + 1, :] = v
    for d in far:
        send(stz.at[z], stz.at[z], ssem.at[4], misc.at[3], dev(x, c, y, zp(d)))
    for u in range(2, 2 * RING - 2):
        ring(u)
    arrive(stz.at[pl.ds(0, nz - 1)], misc.at[3])
    m1, m2, s1, s2, s12 = combine(stz, nz, float(group))
    i1 = lax.rsqrt(s1 / all_rows + epsilon)
    i2 = lax.rsqrt(s2 / all_rows + epsilon)
    mine = c * n + y
    for r, v in enumerate((m1, m2, i1, i2, s12 * i1 * i2 / all_rows)):
        mr[mine, r:r + 1, :] = v
    for dc in range(2):
        for d in range(n):
            if d or dc:
                send(mr.at[mine], mr.at[mine], ssem.at[5], misc.at[4], dev(x, lax.rem(c + dc, 2), yp(d), z))
    ring(2 * RING - 2)
    ring(2 * RING - 1)
    arrive(mr.at[pl.ds(0, 2 * n - 1)], misc.at[4])
    first = c == 0
    for q in range(2 * n):
        cols = slice(q * LANE, (q + 1) * LANE)
        for r, (u, v) in enumerate(((0, 1), (2, 3), (4, 4))):
            coef[r:r + 1, cols] = jnp.where(first, mr[q, u:u + 1, :], mr[q, v:v + 1, :])

    def standard(raw, h):
        cols = slice(h * COLS, (h + 1) * COLS)
        return (raw.astype(f32) - coef[0:1, cols]) * coef[1:2, cols]

    arrive(lraw.at[pl.ds(0, n - 1)], misc.at[2])
    for q in range(n):
        for i in range(2 * np):
            h, r = i // np, i % np
            nl[q * rows + r * hr:q * rows + (r + 1) * hr, h * COLS:(h + 1) * COLS] = standard(
                lraw[q, i], h
            ).astype(bf16)

    def normalize(block, to, start):
        for i in range(2 * np):
            h, r = i // np, i % np
            lines = slice(start + r * hr, start + (r + 1) * hr)
            nr[to, lines, h * COLS:(h + 1) * COLS] = standard(gath[block, i], h).astype(bf16)

    def multiply(p):
        start = (p % 2) * 2 * rows
        normalize(zp(-p), p // 2, start)
        normalize(zp(p + 1), p // 2, start + rows)
        ksend[p] = lax.dot_general(
            nl[...], nr[p // 2, start:start + 2 * rows, :], (((1,), (1,)), ((), ())),
            preferred_element_type=f32,
        ).astype(bf16).reshape(n, rows, 2 * rows)
        for d in range(1, n):
            send(ksend.at[p, xp(d)], arecv.at[p, d - 1], ssem.at[6], asem.at[p], dev(xp(d), c, y, z))

    def last(k):
        start = (2 + k) * rows
        normalize(zp(1 - half) if k == 0 else zp(half), half // 2 - 1, start)
        klast[k] = lax.dot_general(
            nr[half // 2 - 1, start:start + rows, :], nl[...], (((1,), (1,)), ((), ())),
            preferred_element_type=f32,
        ).astype(bf16)
        for d in range(n):
            send(klast.at[k], kall.at[k, x], ssem.at[8], lastsem.at[k], dev(xp(d), 1 - c, y, z))

    def reduce(p):
        place = pl.ds((p % 2) * 2 * rows, 2 * rows)
        arrive(arecv.at[p], asem.at[p])
        s = ksend[p, x].astype(f32)
        for d in range(n - 1):
            s += arecv[p, d].astype(f32)
        dsend[p] = s.astype(bf16)
        for d in range(n):
            send(
                dsend.at[p], kfull.at[p // 2, x, :, place], ssem.at[7], dsem.at[p // 2],
                dev(xp(d), 1 - c, y, z),
            )

    def consume(two):
        arrive(kfull.at[two], dsem.at[two])
        acc[...] += jnp.dot(
            kfull[two].reshape(group, 4 * rows), nr[two], preferred_element_type=f32
        ).reshape(n, rows, width)

    def finish(p):
        here = half // 2 - 1
        if p == half - 2:
            arrive(kfull.at[here, :, :, pl.ds(0, 2 * rows)], dsem.at[here])
            product = jnp.dot(
                kfull[here, :, :, 0:2 * rows].reshape(group, 2 * rows), nr[here, 0:2 * rows, :],
                preferred_element_type=f32,
            )
        else:
            parts = []
            for k in range(2):
                arrive(kall.at[k], lastsem.at[k])
                v = kall[k, 0].astype(f32)
                for d in range(1, n):
                    v += kall[k, d].astype(f32)
                parts.append(v.astype(bf16))
            product = lax.dot_general(
                jnp.concatenate(parts, axis=0), nr[here, 2 * rows:4 * rows, :],
                (((0,), (0,)), ((), ())), preferred_element_type=f32,
            )
        acc[...] += product.reshape(n, rows, width)

    for work, p in (
        (ring, 8), (multiply, 0), (ring, 9), (multiply, 1), (ring, 10), (multiply, 2),
        (ring, 11), (multiply, 3), (reduce, 0), (ring, 12), (reduce, 1), (ring, 13),
        (multiply, 4), (multiply, 5), (ring, 14), (reduce, 2), (reduce, 3), (ring, 15),
        (multiply, 6), (last, 0), (consume, 0), (reduce, 4), (reduce, 5), (ring, 16), (ring, 17),
        (last, 1), (reduce, 6), (consume, 1), (consume, 2), (finish, 6), (finish, 7),
    ):
        work(p)

    plain = jnp.zeros((1, width), f32)
    times = jnp.zeros((1, width), f32)
    for q in range(n):
        v = acc[q]
        plain += jnp.sum(v, axis=0, keepdims=True)
        times += jnp.sum(v * nl[q * rows:(q + 1) * rows, :].astype(f32), axis=0, keepdims=True)
    tl[z, 0:1, :] = plain
    tl[z, 1:2, :] = times
    for d in far:
        send(tl.at[z], tl.at[z], ssem.at[9], misc.at[5], dev(x, c, y, zp(d)))
    for q in range(n):
        for h in range(2):
            ysend[q, h] = acc[q, :, h * COLS:(h + 1) * COLS].astype(bf16)
    row = [(dc, d) for dc in range(2) for d in range(n)][1:]
    for dc, d in row:
        cc, yy = lax.rem(c + dc, 2), yp(d)
        send(ysend.at[yy, cc], yrecv.at[c * n + y], ssem.at[10], misc.at[6], dev(x, cc, yy, z))
    yrecv[c * n + y] = ysend[y, c]
    arrive(tl.at[pl.ds(0, nz - 1)], misc.at[5])
    sums = tl[0]
    for q in range(1, nz):
        sums += tl[q]
    for h in range(2):
        tsend[h] = sums[:, h * COLS:(h + 1) * COLS]
    for dc, d in row:
        cc, yy = lax.rem(c + dc, 2), yp(d)
        send(tsend.at[cc], ty.at[c * n + y], ssem.at[11], misc.at[7], dev(x, cc, yy, z))
    ty[c * n + y] = tsend[c]
    diagonal = coef[2:3, :]
    terms = ((1.0 - diagonal) * (1.0 - diagonal) - off_weight * diagonal * diagonal) / n + (
        off_weight / (all_rows * all_rows)
    ) * sums[1:2, :]
    place = t * n + y
    lbx[place] = jnp.broadcast_to(
        jnp.sum(terms, axis=1, keepdims=True) * (0.5 / features), (1, LANE)
    )
    for dx, dc, dy in plane:
        to = dev(xp(dx), lax.rem(c + dc, 2), yp(dy), z)
        send(lbx.at[place], lbx.at[place], ssem.at[12], misc.at[8], to)

    scale = 2.0 * off_weight / all_rows
    for q in range(n):
        cols = slice(q * LANE, (q + 1) * LANE)
        for r in range(5):
            params[r:r + 1, cols] = mr[c * n + q, r:r + 1, :]
    diagonal = params[4:5, :]
    lead = -2.0 * (1.0 - diagonal) - 2.0 * off_weight * diagonal
    hats = [
        (own[v, c].astype(f32) - params[v:v + 1, :]) * params[2 + v:3 + v, :] for v in range(2)
    ]
    arrive(yrecv.at[pl.ds(0, 2 * n - 1)], misc.at[6])
    arrive(ty.at[pl.ds(0, 2 * n - 1)], misc.at[7])
    for v, out in enumerate((o1, o2)):
        product = yrecv[v * n].astype(f32)
        sums = ty[v * n]
        for q in range(1, n):
            product += yrecv[v * n + q].astype(f32)
            sums += ty[v * n + q]
        sums = sums * (scale / all_rows)
        back = scale * product + lead * hats[1 - v]
        g = back - sums[0:1, :] - hats[v] * (sums[1:2, :] + lead * diagonal)
        out[...] = (g * params[2 + v:3 + v, :]).astype(bf16)
    arrive(lbx.at[pl.ds(0, 2 * n * n - 1)], misc.at[8])
    part = lbx[0]
    for q in range(1, 2 * n * n):
        part += lbx[q]
    loss_ref[...] = part

    arrive(own.at[0, 0], ssem.at[0])
    arrive(sty.at[pl.ds(0, n - 1)], ssem.at[1])
    arrive(gath.at[pl.ds(0, nz - 1)], ssem.at[2])
    arrive(lraw.at[pl.ds(0, n - 1)], ssem.at[3])
    arrive(stz.at[pl.ds(0, nz - 1)], ssem.at[4])
    arrive(mr.at[pl.ds(0, 2 * n - 1)], ssem.at[5])
    arrive(arecv, ssem.at[6])
    arrive(ksend, ssem.at[7])
    arrive(kall, ssem.at[8])
    arrive(tl.at[pl.ds(0, nz - 1)], ssem.at[9])
    arrive(yrecv.at[pl.ds(0, 2 * n - 1)], ssem.at[10])
    arrive(ty.at[pl.ds(0, 2 * n - 1)], ssem.at[11])
    arrive(lbx.at[pl.ds(0, 2 * n * n - 1)], ssem.at[12])


def local(first_view_output, second_view_output):
    n, nz, rows = SIDE, DEPTH, ROWS
    group, width, half, np = n * rows, 2 * COLS, nz // 2, PIECES // 2
    shape = first_view_output.shape
    vmem = pl.BlockSpec(memory_space=pltpu.VMEM)
    dma = pltpu.SemaphoreType.DMA
    g1, g2, loss = pl.pallas_call(
        kernel,
        out_shape=(
            jax.ShapeDtypeStruct(shape, bf16),
            jax.ShapeDtypeStruct(shape, bf16),
            jax.ShapeDtypeStruct((1, LANE), f32),
        ),
        in_specs=[pl.BlockSpec(memory_space=pltpu.HBM)] * 2,
        out_specs=(vmem,) * 3,
        scratch_shapes=[
            pltpu.VMEM((2, 2, rows, COLS), bf16),
            pltpu.VMEM((nz, 2 * np, rows // np, COLS), bf16),
            pltpu.VMEM((n, 2 * np, rows // np, COLS), bf16),
            pltpu.VMEM((group, width), bf16),
            pltpu.VMEM((half // 2, 4 * rows, width), bf16),
            pltpu.VMEM((n, 5, LANE), f32),
            pltpu.VMEM((n, 5, LANE), f32),
            pltpu.VMEM((nz, 5, LANE), f32),
            pltpu.VMEM((2 * n, 5, LANE), f32),
            pltpu.VMEM((8, width), f32),
            pltpu.VMEM((half - 1, n, rows, 2 * rows), bf16),
            pltpu.VMEM((half - 1, n - 1, rows, 2 * rows), bf16),
            pltpu.VMEM((half - 1, rows, 2 * rows), bf16),
            pltpu.VMEM((half // 2, n, rows, 4 * rows), bf16),
            pltpu.VMEM((2, rows, group), bf16),
            pltpu.VMEM((2, n, rows, group), bf16),
            pltpu.VMEM((n, rows, width), f32),
            pltpu.VMEM((nz, 2, width), f32),
            pltpu.VMEM((2, 2, COLS), f32),
            pltpu.VMEM((2 * n, 2, COLS), f32),
            pltpu.VMEM((n, 2, rows, COLS), bf16),
            pltpu.VMEM((2 * n, rows, COLS), bf16),
            pltpu.VMEM((8, COLS), f32),
            pltpu.VMEM((2 * n * n, 1, LANE), f32),
            dma((13,)), dma((9,)), dma((2, half, PIECES)), dma((half,)), dma((half,)), dma((2,)), dma((2,)),
        ],
        compiler_params=pltpu.CompilerParams(
            collective_id=0, has_side_effects=True, vmem_limit_bytes=40 * 2**20
        ),
    )(first_view_output, second_view_output)
    return g1, g2, loss[0, 0]


def solution(mesh):
    spec = P("batch", "tile")
    return jax.shard_map(
        local, mesh=mesh, in_specs=(spec, spec), out_specs=(spec, spec, P()), check_vma=False
    )
```

```python
import jax
import jax.numpy as jnp
from jax import lax
from jax.experimental import pallas as pl
from jax.experimental.pallas import tpu as pltpu
from jax.sharding import PartitionSpec as P

epsilon = 1e-05
off_weight = 0.0051
SIDE = 4
DEPTH = 16
ROWS = 64
COLS = 512
LANE = 128
PIECES = 4
RING = 4
MESH = pl.DeviceIdType.MESH
f32, bf16 = jnp.float32, jnp.bfloat16


def kernel(
    x1, x2, o1, o2, loss_ref,
    own, gath, lraw, nl, nr, stl, sty, stz, mr, coef,
    ksend, arecv, dsend, kfull, klast, kall, acc, tl, tsend, ty, ysend, yrecv, params, lbx,
    ssem, misc, grecv, asem, dsem, lsem, lastsem,
):
    n, nz, rows = SIDE, DEPTH, ROWS
    np = PIECES // 2
    hr = rows // np
    group = n * rows
    width = 2 * COLS
    half = nz // 2
    all_rows = float(group * nz)
    features = float(n * width)
    b, t = lax.axis_index("batch"), lax.axis_index("tile")
    y, z = b // nz, lax.rem(b, nz)
    x, c = t // 2, lax.rem(t, 2)

    def dev(x, c, y, z):
        return (y * nz + z, x * 2 + c)

    def xp(d):
        return lax.rem(x + d, n)

    def yp(d):
        return lax.rem(y + d, n)

    def zp(d):
        return lax.rem(z + d + nz, nz)

    def send(src, dst, out, into, to):
        pltpu.make_async_remote_copy(
            src_ref=src, dst_ref=dst, send_sem=out, recv_sem=into,
            device_id=to, device_id_type=MESH,
        ).start()

    def arrive(ref, sem):
        pltpu.make_async_copy(ref, ref, sem).wait()

    far = sorted(range(1, nz), key=lambda d: -min(d, nz - d))
    side = sorted(range(n), key=lambda d: -min(d, n - d))

    barrier = pltpu.get_barrier_semaphore()
    peers = 0
    for d in far:
        pl.semaphore_signal(barrier, 1, device_id=dev(x, c, y, zp(d)), device_id_type=MESH)
        peers += 1
    plane = [(dx, dc, dy) for dx in side for dy in side for dc in (1, 0)][:-1]
    for dx, dc, dy in plane:
        to = dev(xp(dx), lax.rem(c + dc, 2), yp(dy), z)
        pl.semaphore_signal(barrier, 1, device_id=to, device_id_type=MESH)
        peers += 1
    loads = [pltpu.make_async_copy(ref, own.at[v, c], lsem.at[v]) for v, ref in enumerate((x1, x2))]
    for load in loads:
        load.start()
    acc[...] = jnp.zeros_like(acc)

    for load in loads:
        load.wait()
    for r in range(np):
        gath[z, np * c + r] = own[c, c, r * hr:(r + 1) * hr, :]
    for q in range(n):
        cols = slice(q * LANE, (q + 1) * LANE)
        v1 = own[0, c, :, cols].astype(f32)
        v2 = own[1, c, :, cols].astype(f32)
        a1 = jnp.sum(v1, axis=0, keepdims=True) / rows
        a2 = jnp.sum(v2, axis=0, keepdims=True) / rows
        v1, v2 = v1 - a1, v2 - a2
        stl[q, 0:1, :] = a1
        stl[q, 1:2, :] = a2
        stl[q, 2:3, :] = jnp.sum(v1 * v1, axis=0, keepdims=True)
        stl[q, 3:4, :] = jnp.sum(v2 * v2, axis=0, keepdims=True)
        stl[q, 4:5, :] = jnp.sum(v1 * v2, axis=0, keepdims=True)
    sty[y] = stl[y]
    pl.semaphore_wait(barrier, peers)

    def block_of(way, s):
        return zp(-s) if way == 0 else zp(s)

    def piece(i):
        return lax.rem(np * c + i, 2 * np)

    def forward(way, s, i):
        part = gath.at[block_of(way, s), piece(i)]
        to = zp(1) if way == 0 else zp(-1)
        send(part, part, ssem.at[2], grecv.at[way, s, i], dev(x, c, y, to))

    def ring(u):
        s, g = u // 2, u % 2
        for k in range(np):
            i = np * g + k
            for way in range(2):
                last = half - g if way == 0 else half - 1 + g

                @pl.when(s <= last)
                def _():
                    arrive(gath.at[block_of(way, s), piece(i)], grecv.at[way, s - 1, i])

                @pl.when(s <= last - 1)
                def _():
                    forward(way, s, i)

    send(own.at[1 - c, c], own.at[1 - c, c], ssem.at[0], misc.at[0], dev(x, 1 - c, y, z))
    for i in range(np):
        for way in range(2):
            forward(way, 0, i)
    for d in side[:-1]:
        send(stl.at[yp(d)], sty.at[y], ssem.at[1], misc.at[1], dev(x, c, yp(d), z))
    arrive(own.at[0, 0], misc.at[0])
    for r in range(np):
        gath[z, np * (1 - c) + r] = own[c, 1 - c, r * hr:(r + 1) * hr, :]
    for i in range(np, 2 * np):
        for way in range(2):
            forward(way, 0, i)
    for d in range(1, n):
        send(gath.at[z], lraw.at[y], ssem.at[3], misc.at[2], dev(x, c, yp(d), z))
    for i in range(2 * np):
        lraw[y, i] = gath[z, i]

    def combine(ref, parts, count):
        means = ref[0, 0:2, :]
        for q in range(1, parts):
            means += ref[q, 0:2, :]
        means = means / parts
        m1, m2 = means[0:1, :], means[1:2, :]
        s1 = s2 = s12 = jnp.zeros((1, LANE), f32)
        for q in range(parts):
            d1, d2 = ref[q, 0:1, :] - m1, ref[q, 1:2, :] - m2
            s1 += ref[q, 2:3, :] + count * (d1 * d1)
            s2 += ref[q, 3:4, :] + count * (d2 * d2)
            s12 += ref[q, 4:5, :] + count * (d1 * d2)
        return m1, m2, s1, s2, s12

    arrive(sty.at[pl.ds(0, n - 1)], misc.at[1])
    for r, v in enumerate(combine(sty, n, float(rows))):
        stz[z, r:r + 1, :] = v
    for d in far:
        send(stz.at[z], stz.at[z], ssem.at[4], misc.at[3], dev(x, c, y, zp(d)))
    for u in range(2, 2 * RING - 2):
        ring(u)
    arrive(stz.at[pl.ds(0, nz - 1)], misc.at[3])
    m1, m2, s1, s2, s12 = combine(stz, nz, float(group))
    i1 = lax.rsqrt(s1 / all_rows + epsilon)
    i2 = lax.rsqrt(s2 / all_rows + epsilon)
    mine = c * n + y
    for r, v in enumerate((m1, m2, i1, i2, s12 * i1 * i2 / all_rows)):
        mr[mine, r:r + 1, :] = v
    row = [(dc, d) for d in side for dc in (1, 0)][:-1]
    for dc, d in row:
        send(mr.at[mine], mr.at[mine], ssem.at[5], misc.at[4], dev(x, lax.rem(c + dc, 2), yp(d), z))
    ring(2 * RING - 2)
    ring(2 * RING - 1)
    arrive(mr.at[pl.ds(0, 2 * n - 1)], misc.at[4])
    first = c == 0
    for q in range(2 * n):
        cols = slice(q * LANE, (q + 1) * LANE)
        for r, (u, v) in enumerate(((0, 1), (2, 3), (4, 4))):
            coef[r:r + 1, cols] = jnp.where(first, mr[q, u:u + 1, :], mr[q, v:v + 1, :])

    def standard(raw, h):
        cols = slice(h * COLS, (h + 1) * COLS)
        return (raw.astype(f32) - coef[0:1, cols]) * coef[1:2, cols]

    arrive(lraw.at[pl.ds(0, n - 1)], misc.at[2])
    for q in range(n):
        for i in range(2 * np):
            h, r = i // np, i % np
            nl[q * rows + r * hr:q * rows + (r + 1) * hr, h * COLS:(h + 1) * COLS] = standard(
                lraw[q, i], h
            ).astype(bf16)

    def normalize(block, to, start):
        for i in range(2 * np):
            h, r = i // np, i % np
            lines = slice(start + r * hr, start + (r + 1) * hr)
            nr[to, lines, h * COLS:(h + 1) * COLS] = standard(gath[block, i], h).astype(bf16)

    def multiply(p):
        start = (p % 2) * 2 * rows
        normalize(zp(-p), p // 2, start)
        normalize(zp(p + 1), p // 2, start + rows)
        ksend[p] = lax.dot_general(
            nl[...], nr[p // 2, start:start + 2 * rows, :], (((1,), (1,)), ((), ())),
            preferred_element_type=f32,
        ).astype(bf16).reshape(n, rows, 2 * rows)
        for d in side[:-1]:
            send(ksend.at[p, xp(d)], arecv.at[p, d - 1], ssem.at[6], asem.at[p], dev(xp(d), c, y, z))

    def last(k):
        start = (2 + k) * rows
        normalize(zp(1 - half) if k == 0 else zp(half), half // 2 - 1, start)
        klast[k] = lax.dot_general(
            nr[half // 2 - 1, start:start + rows, :], nl[...], (((1,), (1,)), ((), ())),
            preferred_element_type=f32,
        ).astype(bf16)
        for d in side:
            send(klast.at[k], kall.at[k, x], ssem.at[8], lastsem.at[k], dev(xp(d), 1 - c, y, z))

    def reduce(p):
        place = pl.ds((p % 2) * 2 * rows, 2 * rows)
        arrive(arecv.at[p], asem.at[p])
        s = ksend[p, x].astype(f32)
        for d in range(n - 1):
            s += arecv[p, d].astype(f32)
        dsend[p] = s.astype(bf16)
        for d in side:
            send(
                dsend.at[p], kfull.at[p // 2, x, :, place], ssem.at[7], dsem.at[p // 2],
                dev(xp(d), 1 - c, y, z),
            )

    def consume(two):
        arrive(kfull.at[two], dsem.at[two])
        acc[...] += jnp.dot(
            kfull[two].reshape(group, 4 * rows), nr[two], preferred_element_type=f32
        ).reshape(n, rows, width)

    def finish(p):
        here = half // 2 - 1
        if p == half - 2:
            arrive(kfull.at[here, :, :, pl.ds(0, 2 * rows)], dsem.at[here])
            product = jnp.dot(
                kfull[here, :, :, 0:2 * rows].reshape(group, 2 * rows), nr[here, 0:2 * rows, :],
                preferred_element_type=f32,
            )
        else:
            parts = []
            for k in range(2):
                arrive(kall.at[k], lastsem.at[k])
                v = kall[k, 0].astype(f32)
                for d in range(1, n):
                    v += kall[k, d].astype(f32)
                parts.append(v.astype(bf16))
            product = lax.dot_general(
                jnp.concatenate(parts, axis=0), nr[here, 2 * rows:4 * rows, :],
                (((0,), (0,)), ((), ())), preferred_element_type=f32,
            )
        acc[...] += product.reshape(n, rows, width)

    for work, p in (
        (ring, 8), (multiply, 0), (ring, 9), (multiply, 1), (ring, 10), (multiply, 2),
        (ring, 11), (multiply, 3), (reduce, 0), (ring, 12), (reduce, 1), (ring, 13),
        (multiply, 4), (multiply, 5), (ring, 14), (reduce, 2), (reduce, 3), (ring, 15),
        (multiply, 6), (last, 0), (consume, 0), (reduce, 4), (reduce, 5), (ring, 16), (ring, 17),
        (last, 1), (reduce, 6), (consume, 1), (consume, 2), (finish, 6), (finish, 7),
    ):
        work(p)

    plain = jnp.zeros((1, width), f32)
    times = jnp.zeros((1, width), f32)
    for q in range(n):
        v = acc[q]
        plain += jnp.sum(v, axis=0, keepdims=True)
        times += jnp.sum(v * nl[q * rows:(q + 1) * rows, :].astype(f32), axis=0, keepdims=True)
    tl[z, 0:1, :] = plain
    tl[z, 1:2, :] = times
    for d in far:
        send(tl.at[z], tl.at[z], ssem.at[9], misc.at[5], dev(x, c, y, zp(d)))
    for q in range(n):
        for h in range(2):
            ysend[q, h] = acc[q, :, h * COLS:(h + 1) * COLS].astype(bf16)
    for dc, d in row:
        cc, yy = lax.rem(c + dc, 2), yp(d)
        send(ysend.at[yy, cc], yrecv.at[c * n + y], ssem.at[10], misc.at[6], dev(x, cc, yy, z))
    yrecv[c * n + y] = ysend[y, c]
    arrive(tl.at[pl.ds(0, nz - 1)], misc.at[5])
    sums = tl[0]
    for q in range(1, nz):
        sums += tl[q]
    for h in range(2):
        tsend[h] = sums[:, h * COLS:(h + 1) * COLS]
    for dc, d in row:
        cc, yy = lax.rem(c + dc, 2), yp(d)
        send(tsend.at[cc], ty.at[c * n + y], ssem.at[11], misc.at[7], dev(x, cc, yy, z))
    ty[c * n + y] = tsend[c]
    diagonal = coef[2:3, :]
    terms = ((1.0 - diagonal) * (1.0 - diagonal) - off_weight * diagonal * diagonal) / n + (
        off_weight / (all_rows * all_rows)
    ) * sums[1:2, :]
    place = t * n + y
    lbx[place] = jnp.broadcast_to(
        jnp.sum(terms, axis=1, keepdims=True) * (0.5 / features), (1, LANE)
    )
    for dx, dc, dy in plane:
        to = dev(xp(dx), lax.rem(c + dc, 2), yp(dy), z)
        send(lbx.at[place], lbx.at[place], ssem.at[12], misc.at[8], to)

    scale = 2.0 * off_weight / all_rows
    for q in range(n):
        cols = slice(q * LANE, (q + 1) * LANE)
        for r in range(5):
            params[r:r + 1, cols] = mr[c * n + q, r:r + 1, :]
    diagonal = params[4:5, :]
    lead = -2.0 * (1.0 - diagonal) - 2.0 * off_weight * diagonal
    hats = [
        (own[v, c].astype(f32) - params[v:v + 1, :]) * params[2 + v:3 + v, :] for v in range(2)
    ]
    arrive(yrecv.at[pl.ds(0, 2 * n - 1)], misc.at[6])
    arrive(ty.at[pl.ds(0, 2 * n - 1)], misc.at[7])
    for v, out in enumerate((o1, o2)):
        product = yrecv[v * n].astype(f32)
        sums = ty[v * n]
        for q in range(1, n):
            product += yrecv[v * n + q].astype(f32)
            sums += ty[v * n + q]
        sums = sums * (scale / all_rows)
        back = scale * product + lead * hats[1 - v]
        g = back - sums[0:1, :] - hats[v] * (sums[1:2, :] + lead * diagonal)
        out[...] = (g * params[2 + v:3 + v, :]).astype(bf16)
    arrive(lbx.at[pl.ds(0, 2 * n * n - 1)], misc.at[8])
    part = lbx[0]
    for q in range(1, 2 * n * n):
        part += lbx[q]
    loss_ref[...] = part

    arrive(own.at[0, 0], ssem.at[0])
    arrive(sty.at[pl.ds(0, n - 1)], ssem.at[1])
    arrive(gath.at[pl.ds(0, nz - 1)], ssem.at[2])
    arrive(lraw.at[pl.ds(0, n - 1)], ssem.at[3])
    arrive(stz.at[pl.ds(0, nz - 1)], ssem.at[4])
    arrive(mr.at[pl.ds(0, 2 * n - 1)], ssem.at[5])
    arrive(arecv, ssem.at[6])
    arrive(ksend, ssem.at[7])
    arrive(kall, ssem.at[8])
    arrive(tl.at[pl.ds(0, nz - 1)], ssem.at[9])
    arrive(yrecv.at[pl.ds(0, 2 * n - 1)], ssem.at[10])
    arrive(ty.at[pl.ds(0, 2 * n - 1)], ssem.at[11])
    arrive(lbx.at[pl.ds(0, 2 * n * n - 1)], ssem.at[12])


def local(first_view_output, second_view_output):
    n, nz, rows = SIDE, DEPTH, ROWS
    group, width, half, np = n * rows, 2 * COLS, nz // 2, PIECES // 2
    shape = first_view_output.shape
    vmem = pl.BlockSpec(memory_space=pltpu.VMEM)
    dma = pltpu.SemaphoreType.DMA
    g1, g2, loss = pl.pallas_call(
        kernel,
        out_shape=(
            jax.ShapeDtypeStruct(shape, bf16),
            jax.ShapeDtypeStruct(shape, bf16),
            jax.ShapeDtypeStruct((1, LANE), f32),
        ),
        in_specs=[pl.BlockSpec(memory_space=pltpu.HBM)] * 2,
        out_specs=(vmem,) * 3,
        scratch_shapes=[
            pltpu.VMEM((2, 2, rows, COLS), bf16),
            pltpu.VMEM((nz, 2 * np, rows // np, COLS), bf16),
            pltpu.VMEM((n, 2 * np, rows // np, COLS), bf16),
            pltpu.VMEM((group, width), bf16),
            pltpu.VMEM((half // 2, 4 * rows, width), bf16),
            pltpu.VMEM((n, 5, LANE), f32),
            pltpu.VMEM((n, 5, LANE), f32),
            pltpu.VMEM((nz, 5, LANE), f32),
            pltpu.VMEM((2 * n, 5, LANE), f32),
            pltpu.VMEM((8, width), f32),
            pltpu.VMEM((half - 1, n, rows, 2 * rows), bf16),
            pltpu.VMEM((half - 1, n - 1, rows, 2 * rows), bf16),
            pltpu.VMEM((half - 1, rows, 2 * rows), bf16),
            pltpu.VMEM((half // 2, n, rows, 4 * rows), bf16),
            pltpu.VMEM((2, rows, group), bf16),
            pltpu.VMEM((2, n, rows, group), bf16),
            pltpu.VMEM((n, rows, width), f32),
            pltpu.VMEM((nz, 2, width), f32),
            pltpu.VMEM((2, 2, COLS), f32),
            pltpu.VMEM((2 * n, 2, COLS), f32),
            pltpu.VMEM((n, 2, rows, COLS), bf16),
            pltpu.VMEM((2 * n, rows, COLS), bf16),
            pltpu.VMEM((8, COLS), f32),
            pltpu.VMEM((2 * n * n, 1, LANE), f32),
            dma((13,)), dma((9,)), dma((2, half, PIECES)), dma((half,)), dma((half,)), dma((2,)), dma((2,)),
        ],
        compiler_params=pltpu.CompilerParams(
            collective_id=0, has_side_effects=True, vmem_limit_bytes=40 * 2**20
        ),
    )(first_view_output, second_view_output)
    return g1, g2, loss[0, 0]


def solution(mesh):
    spec = P("batch", "tile")
    return jax.shard_map(
        local, mesh=mesh, in_specs=(spec, spec), out_specs=(spec, spec, P()), check_vma=False
    )
```

```python
import jax
import jax.numpy as jnp
from jax import lax
from jax.experimental import pallas as pl
from jax.experimental.pallas import tpu as pltpu
from jax.sharding import PartitionSpec as P

epsilon = 1e-05
off_weight = 0.0051
SIDE = 4
DEPTH = 16
ROWS = 64
COLS = 512
LANE = 128
PIECES = 4
RING = 4
MESH = pl.DeviceIdType.MESH
f32, bf16 = jnp.float32, jnp.bfloat16


def kernel(
    x1, x2, o1, o2, loss_ref,
    own, gath, lraw, nl, nr, stl, sty, stz, mr, coef,
    ksend, arecv, dsend, kfull, klast, kall, acc, tl, tsend, ty, ysend, yrecv, params, hats, back, lbx,
    ssem, misc, grecv, asem, dsem, lsem, lastsem,
):
    n, nz, rows = SIDE, DEPTH, ROWS
    np = PIECES // 2
    hr = rows // np
    group = n * rows
    width = 2 * COLS
    half = nz // 2
    all_rows = float(group * nz)
    features = float(n * width)
    b, t = lax.axis_index("batch"), lax.axis_index("tile")
    y, z = b // nz, lax.rem(b, nz)
    x, c = t // 2, lax.rem(t, 2)

    def dev(x, c, y, z):
        return (y * nz + z, x * 2 + c)

    def xp(d):
        return lax.rem(x + d, n)

    def yp(d):
        return lax.rem(y + d, n)

    def zp(d):
        return lax.rem(z + d + nz, nz)

    def send(src, dst, out, into, to):
        pltpu.make_async_remote_copy(
            src_ref=src, dst_ref=dst, send_sem=out, recv_sem=into,
            device_id=to, device_id_type=MESH,
        ).start()

    def arrive(ref, sem):
        pltpu.make_async_copy(ref, ref, sem).wait()

    far = sorted(range(1, nz), key=lambda d: -min(d, nz - d))
    side = sorted(range(n), key=lambda d: -min(d, n - d))

    barrier = pltpu.get_barrier_semaphore()
    peers = 0
    for d in far:
        pl.semaphore_signal(barrier, 1, device_id=dev(x, c, y, zp(d)), device_id_type=MESH)
        peers += 1
    plane = [(dx, dc, dy) for dx in side for dy in side for dc in (1, 0)][:-1]
    for dx, dc, dy in plane:
        to = dev(xp(dx), lax.rem(c + dc, 2), yp(dy), z)
        pl.semaphore_signal(barrier, 1, device_id=to, device_id_type=MESH)
        peers += 1
    loads = [pltpu.make_async_copy(ref, own.at[v, c], lsem.at[v]) for v, ref in enumerate((x1, x2))]
    for load in loads:
        load.start()
    acc[...] = jnp.zeros_like(acc)

    for load in loads:
        load.wait()
    for r in range(np):
        gath[z, np * c + r] = own[c, c, r * hr:(r + 1) * hr, :]
    for q in range(n):
        cols = slice(q * LANE, (q + 1) * LANE)
        v1 = own[0, c, :, cols].astype(f32)
        v2 = own[1, c, :, cols].astype(f32)
        a1 = jnp.sum(v1, axis=0, keepdims=True) / rows
        a2 = jnp.sum(v2, axis=0, keepdims=True) / rows
        v1, v2 = v1 - a1, v2 - a2
        stl[q, 0:1, :] = a1
        stl[q, 1:2, :] = a2
        stl[q, 2:3, :] = jnp.sum(v1 * v1, axis=0, keepdims=True)
        stl[q, 3:4, :] = jnp.sum(v2 * v2, axis=0, keepdims=True)
        stl[q, 4:5, :] = jnp.sum(v1 * v2, axis=0, keepdims=True)
    sty[y] = stl[y]
    pl.semaphore_wait(barrier, peers)

    def block_of(way, s):
        return zp(-s) if way == 0 else zp(s)

    def piece(i):
        return lax.rem(np * c + i, 2 * np)

    def forward(way, s, i):
        part = gath.at[block_of(way, s), piece(i)]
        to = zp(1) if way == 0 else zp(-1)
        send(part, part, ssem.at[2], grecv.at[way, s, i], dev(x, c, y, to))

    def ring(u):
        s, g = u // 2, u % 2
        for k in range(np):
            i = np * g + k
            for way in range(2):
                last = half - g if way == 0 else half - 1 + g

                @pl.when(s <= last)
                def _():
                    arrive(gath.at[block_of(way, s), piece(i)], grecv.at[way, s - 1, i])

                @pl.when(s <= last - 1)
                def _():
                    forward(way, s, i)

    send(own.at[1 - c, c], own.at[1 - c, c], ssem.at[0], misc.at[0], dev(x, 1 - c, y, z))
    for i in range(np):
        for way in range(2):
            forward(way, 0, i)
    for d in side[:-1]:
        send(stl.at[yp(d)], sty.at[y], ssem.at[1], misc.at[1], dev(x, c, yp(d), z))
    arrive(own.at[0, 0], misc.at[0])
    for r in range(np):
        gath[z, np * (1 - c) + r] = own[c, 1 - c, r * hr:(r + 1) * hr, :]
    for i in range(np, 2 * np):
        for way in range(2):
            forward(way, 0, i)
    for d in range(1, n):
        send(gath.at[z], lraw.at[y], ssem.at[3], misc.at[2], dev(x, c, yp(d), z))
    for i in range(2 * np):
        lraw[y, i] = gath[z, i]

    def combine(ref, parts, count):
        means = ref[0, 0:2, :]
        for q in range(1, parts):
            means += ref[q, 0:2, :]
        means = means / parts
        m1, m2 = means[0:1, :], means[1:2, :]
        s1 = s2 = s12 = jnp.zeros((1, LANE), f32)
        for q in range(parts):
            d1, d2 = ref[q, 0:1, :] - m1, ref[q, 1:2, :] - m2
            s1 += ref[q, 2:3, :] + count * (d1 * d1)
            s2 += ref[q, 3:4, :] + count * (d2 * d2)
            s12 += ref[q, 4:5, :] + count * (d1 * d2)
        return m1, m2, s1, s2, s12

    arrive(sty.at[pl.ds(0, n - 1)], misc.at[1])
    for r, v in enumerate(combine(sty, n, float(rows))):
        stz[z, r:r + 1, :] = v
    for d in far:
        send(stz.at[z], stz.at[z], ssem.at[4], misc.at[3], dev(x, c, y, zp(d)))
    for u in range(2, 2 * RING - 2):
        ring(u)
    arrive(stz.at[pl.ds(0, nz - 1)], misc.at[3])
    m1, m2, s1, s2, s12 = combine(stz, nz, float(group))
    i1 = lax.rsqrt(s1 / all_rows + epsilon)
    i2 = lax.rsqrt(s2 / all_rows + epsilon)
    mine = c * n + y
    for r, v in enumerate((m1, m2, i1, i2, s12 * i1 * i2 / all_rows)):
        mr[mine, r:r + 1, :] = v
    row = [(dc, d) for d in side for dc in (1, 0)][:-1]
    for dc, d in row:
        send(mr.at[mine], mr.at[mine], ssem.at[5], misc.at[4], dev(x, lax.rem(c + dc, 2), yp(d), z))
    ring(2 * RING - 2)
    ring(2 * RING - 1)
    arrive(mr.at[pl.ds(0, 2 * n - 1)], misc.at[4])
    first = c == 0
    for q in range(2 * n):
        cols = slice(q * LANE, (q + 1) * LANE)
        for r, (u, v) in enumerate(((0, 1), (2, 3), (4, 4))):
            coef[r:r + 1, cols] = jnp.where(first, mr[q, u:u + 1, :], mr[q, v:v + 1, :])

    def standard(raw, h):
        cols = slice(h * COLS, (h + 1) * COLS)
        return (raw.astype(f32) - coef[0:1, cols]) * coef[1:2, cols]

    arrive(lraw.at[pl.ds(0, n - 1)], misc.at[2])
    for q in range(n):
        for i in range(2 * np):
            h, r = i // np, i % np
            nl[q * rows + r * hr:q * rows + (r + 1) * hr, h * COLS:(h + 1) * COLS] = standard(
                lraw[q, i], h
            ).astype(bf16)

    def normalize(block, to, start):
        for i in range(2 * np):
            h, r = i // np, i % np
            lines = slice(start + r * hr, start + (r + 1) * hr)
            nr[to, lines, h * COLS:(h + 1) * COLS] = standard(gath[block, i], h).astype(bf16)

    def multiply(p):
        start = (p % 2) * 2 * rows
        normalize(zp(-p), p // 2, start)
        normalize(zp(p + 1), p // 2, start + rows)
        ksend[p] = lax.dot_general(
            nl[...], nr[p // 2, start:start + 2 * rows, :], (((1,), (1,)), ((), ())),
            preferred_element_type=f32,
        ).astype(bf16).reshape(n, rows, 2 * rows)
        for d in side[:-1]:
            send(ksend.at[p, xp(d)], arecv.at[p, d - 1], ssem.at[6], asem.at[p], dev(xp(d), c, y, z))

    def last(k):
        start = (2 + k) * rows
        normalize(zp(1 - half) if k == 0 else zp(half), half // 2 - 1, start)
        klast[k] = lax.dot_general(
            nr[half // 2 - 1, start:start + rows, :], nl[...], (((1,), (1,)), ((), ())),
            preferred_element_type=f32,
        ).astype(bf16)
        for d in side:
            send(klast.at[k], kall.at[k, x], ssem.at[8], lastsem.at[k], dev(xp(d), 1 - c, y, z))

    def reduce(p):
        place = pl.ds((p % 2) * 2 * rows, 2 * rows)
        arrive(arecv.at[p], asem.at[p])
        s = ksend[p, x].astype(f32)
        for d in range(n - 1):
            s += arecv[p, d].astype(f32)
        dsend[p] = s.astype(bf16)
        for d in side:
            send(
                dsend.at[p], kfull.at[p // 2, x, :, place], ssem.at[7], dsem.at[p // 2],
                dev(xp(d), 1 - c, y, z),
            )

    def consume(two):
        arrive(kfull.at[two], dsem.at[two])
        acc[...] += jnp.dot(
            kfull[two].reshape(group, 4 * rows), nr[two], preferred_element_type=f32
        ).reshape(n, rows, width)

    def finish(p):
        here = half // 2 - 1
        if p == half - 2:
            arrive(kfull.at[here, :, :, pl.ds(0, 2 * rows)], dsem.at[here])
            product = jnp.dot(
                kfull[here, :, :, 0:2 * rows].reshape(group, 2 * rows), nr[here, 0:2 * rows, :],
                preferred_element_type=f32,
            )
        else:
            parts = []
            for k in range(2):
                arrive(kall.at[k], lastsem.at[k])
                v = kall[k, 0].astype(f32)
                for d in range(1, n):
                    v += kall[k, d].astype(f32)
                parts.append(v.astype(bf16))
            product = lax.dot_general(
                jnp.concatenate(parts, axis=0), nr[here, 2 * rows:4 * rows, :],
                (((0,), (0,)), ((), ())), preferred_element_type=f32,
            )
        acc[...] += product.reshape(n, rows, width)

    for work, p in (
        (ring, 8), (multiply, 0), (ring, 9), (multiply, 1), (ring, 10), (multiply, 2),
        (ring, 11), (multiply, 3), (reduce, 0), (ring, 12), (reduce, 1), (ring, 13),
        (multiply, 4), (multiply, 5), (ring, 14), (reduce, 2), (reduce, 3), (ring, 15),
        (multiply, 6), (last, 0), (consume, 0), (reduce, 4), (reduce, 5), (ring, 16), (ring, 17),
        (last, 1), (reduce, 6), (consume, 1), (consume, 2), (finish, 6), (finish, 7),
    ):
        work(p)

    plain = jnp.zeros((1, width), f32)
    times = jnp.zeros((1, width), f32)
    for q in range(n):
        v = acc[q]
        plain += jnp.sum(v, axis=0, keepdims=True)
        times += jnp.sum(v * nl[q * rows:(q + 1) * rows, :].astype(f32), axis=0, keepdims=True)
    tl[z, 0:1, :] = plain
    tl[z, 1:2, :] = times
    for d in far:
        send(tl.at[z], tl.at[z], ssem.at[9], misc.at[5], dev(x, c, y, zp(d)))
    for q in range(n):
        for h in range(2):
            ysend[q, h] = acc[q, :, h * COLS:(h + 1) * COLS].astype(bf16)
    for dc, d in row:
        cc, yy = lax.rem(c + dc, 2), yp(d)
        send(ysend.at[yy, cc], yrecv.at[c * n + y], ssem.at[10], misc.at[6], dev(x, cc, yy, z))
    yrecv[c * n + y] = ysend[y, c]
    scale = 2.0 * off_weight / all_rows
    for q in range(n):
        cols = slice(q * LANE, (q + 1) * LANE)
        for r in range(5):
            params[r:r + 1, cols] = mr[c * n + q, r:r + 1, :]
    params[5:6, :] = -2.0 * (1.0 - params[4:5, :]) - 2.0 * off_weight * params[4:5, :]
    params[6:7, :] = params[5:6, :] * params[4:5, :]
    for v in range(2):
        hats[v] = (own[v, c].astype(f32) - params[v:v + 1, :]) * params[2 + v:3 + v, :]
    diagonal = coef[2:3, :]
    coef[3:4, :] = (
        (1.0 - diagonal) * (1.0 - diagonal) - off_weight * diagonal * diagonal
    ) / n
    arrive(tl.at[pl.ds(0, nz - 1)], misc.at[5])
    sums = tl[0]
    for q in range(1, nz):
        sums += tl[q]
    for h in range(2):
        tsend[h] = sums[:, h * COLS:(h + 1) * COLS]
    for dc, d in row:
        cc, yy = lax.rem(c + dc, 2), yp(d)
        send(tsend.at[cc], ty.at[c * n + y], ssem.at[11], misc.at[7], dev(x, cc, yy, z))
    ty[c * n + y] = tsend[c]
    terms = coef[3:4, :] + (off_weight / (all_rows * all_rows)) * sums[1:2, :]
    place = t * n + y
    lbx[place] = jnp.broadcast_to(
        jnp.sum(terms, axis=1, keepdims=True) * (0.5 / features), (1, LANE)
    )
    for dx, dc, dy in plane:
        to = dev(xp(dx), lax.rem(c + dc, 2), yp(dy), z)
        send(lbx.at[place], lbx.at[place], ssem.at[12], misc.at[8], to)

    arrive(yrecv.at[pl.ds(0, 2 * n - 1)], misc.at[6])
    for v in range(2):
        product = yrecv[v * n].astype(f32)
        for q in range(1, n):
            product += yrecv[v * n + q].astype(f32)
        back[v] = scale * product + params[5:6, :] * hats[1 - v]
    arrive(ty.at[pl.ds(0, 2 * n - 1)], misc.at[7])
    for v, out in enumerate((o1, o2)):
        sums = ty[v * n]
        for q in range(1, n):
            sums += ty[v * n + q]
        sums = sums * (scale / all_rows)
        g = back[v] - sums[0:1, :] - hats[v] * (sums[1:2, :] + params[6:7, :])
        out[...] = (g * params[2 + v:3 + v, :]).astype(bf16)
    arrive(lbx.at[pl.ds(0, 2 * n * n - 1)], misc.at[8])
    part = lbx[0]
    for q in range(1, 2 * n * n):
        part += lbx[q]
    loss_ref[...] = part

    arrive(own.at[0, 0], ssem.at[0])
    arrive(sty.at[pl.ds(0, n - 1)], ssem.at[1])
    arrive(gath.at[pl.ds(0, nz - 1)], ssem.at[2])
    arrive(lraw.at[pl.ds(0, n - 1)], ssem.at[3])
    arrive(stz.at[pl.ds(0, nz - 1)], ssem.at[4])
    arrive(mr.at[pl.ds(0, 2 * n - 1)], ssem.at[5])
    arrive(arecv, ssem.at[6])
    arrive(ksend, ssem.at[7])
    arrive(kall, ssem.at[8])
    arrive(tl.at[pl.ds(0, nz - 1)], ssem.at[9])
    arrive(yrecv.at[pl.ds(0, 2 * n - 1)], ssem.at[10])
    arrive(ty.at[pl.ds(0, 2 * n - 1)], ssem.at[11])
    arrive(lbx.at[pl.ds(0, 2 * n * n - 1)], ssem.at[12])


def local(first_view_output, second_view_output):
    n, nz, rows = SIDE, DEPTH, ROWS
    group, width, half, np = n * rows, 2 * COLS, nz // 2, PIECES // 2
    shape = first_view_output.shape
    vmem = pl.BlockSpec(memory_space=pltpu.VMEM)
    dma = pltpu.SemaphoreType.DMA
    g1, g2, loss = pl.pallas_call(
        kernel,
        out_shape=(
            jax.ShapeDtypeStruct(shape, bf16),
            jax.ShapeDtypeStruct(shape, bf16),
            jax.ShapeDtypeStruct((1, LANE), f32),
        ),
        in_specs=[pl.BlockSpec(memory_space=pltpu.HBM)] * 2,
        out_specs=(vmem,) * 3,
        scratch_shapes=[
            pltpu.VMEM((2, 2, rows, COLS), bf16),
            pltpu.VMEM((nz, 2 * np, rows // np, COLS), bf16),
            pltpu.VMEM((n, 2 * np, rows // np, COLS), bf16),
            pltpu.VMEM((group, width), bf16),
            pltpu.VMEM((half // 2, 4 * rows, width), bf16),
            pltpu.VMEM((n, 5, LANE), f32),
            pltpu.VMEM((n, 5, LANE), f32),
            pltpu.VMEM((nz, 5, LANE), f32),
            pltpu.VMEM((2 * n, 5, LANE), f32),
            pltpu.VMEM((8, width), f32),
            pltpu.VMEM((half - 1, n, rows, 2 * rows), bf16),
            pltpu.VMEM((half - 1, n - 1, rows, 2 * rows), bf16),
            pltpu.VMEM((half - 1, rows, 2 * rows), bf16),
            pltpu.VMEM((half // 2, n, rows, 4 * rows), bf16),
            pltpu.VMEM((2, rows, group), bf16),
            pltpu.VMEM((2, n, rows, group), bf16),
            pltpu.VMEM((n, rows, width), f32),
            pltpu.VMEM((nz, 2, width), f32),
            pltpu.VMEM((2, 2, COLS), f32),
            pltpu.VMEM((2 * n, 2, COLS), f32),
            pltpu.VMEM((n, 2, rows, COLS), bf16),
            pltpu.VMEM((2 * n, rows, COLS), bf16),
            pltpu.VMEM((8, COLS), f32),
            pltpu.VMEM((2, rows, COLS), f32),
            pltpu.VMEM((2, rows, COLS), f32),
            pltpu.VMEM((2 * n * n, 1, LANE), f32),
            dma((13,)), dma((9,)), dma((2, half, PIECES)), dma((half,)), dma((half,)), dma((2,)), dma((2,)),
        ],
        compiler_params=pltpu.CompilerParams(
            collective_id=0, has_side_effects=True, vmem_limit_bytes=40 * 2**20
        ),
    )(first_view_output, second_view_output)
    return g1, g2, loss[0, 0]


def solution(mesh):
    spec = P("batch", "tile")
    return jax.shard_map(
        local, mesh=mesh, in_specs=(spec, spec), out_specs=(spec, spec, P()), check_vma=False
    )
```
